512 devices in a mesh: ctx: 64 (over x, z, core), head: 8 (over y).
Axes of the slice: x: 4, y: 8, z: 8, core: 2. Of those that a mesh axis runs over, the one named last changes fastest.
Arguments:
- normed_query_latent: bfloat16 [2, 16, 1536], replicated, may hold values from -48 to 48
- fresh_token_latent: bfloat16 [2, 16, 576], replicated, may hold values from -16 to 16
- prefix_latent_cache: bfloat16 [32768, 576], P('ctx'), may hold values from -18 to 18
- query_up_weight: bfloat16 [1536, 24576], P(None, ('head', 'ctx')), may hold values from -0.15625 to 0.15625
- key_up_weight: bfloat16 [128, 128, 512], P('head', None, 'ctx'), may hold values from -0.5 to 0.5
- value_up_weight: bfloat16 [128, 512, 128], P('head', 'ctx'), may hold values from -0.25 to 0.25
- output_weight: bfloat16 [16384, 7168], P('head', 'ctx'), may hold values from -0.046875 to 0.046875
- adapter_query_down: bfloat16 [8, 1536, 16], replicated, may hold values from -0.15625 to 0.15625
- adapter_query_up: bfloat16 [8, 16, 24576], P(None, None, ('head', 'ctx')), may hold values from -1.5 to 1.5
- adapter_key_down: bfloat16 [8, 512, 16], P(None, 'ctx'), may hold values from -1.5 to 1.5
- adapter_key_up: bfloat16 [8, 16, 16384], P(None, None, 'head'), may hold values from -0.5 to 0.5
- adapter_value_down: bfloat16 [8, 512, 16], P(None, 'ctx'), may hold values from -0.25 to 0.25
- adapter_value_up: bfloat16 [8, 16, 16384], P(None, None, 'head'), may hold values from -1.5 to 1.5
- request_adapter: int32 [16], replicated, may hold values from 0 to 7, as said below
- group_first_request: int32 [8], replicated, may hold values from 0 to 15, as said below
- group_request_count: int32 [8], replicated, may hold values from 1 to 8, as said below
Outputs:
- mixed: bfloat16 [16, 2, 7168], P('head', None, 'ctx')
The draws below stay inside these ranges and needn't reach their ends.
Inputs may be any that keep to these rules, and one draw needn't show every extreme that they name: Requests come ordered by adapter: request_adapter never falls, and the requests of adapter a are exactly rows group_first_request[a] to group_first_request[a] + group_request_count[a] - 1. group_first_request[a] is the number of requests whose adapter is below a. `group_request_count`: every adapter has at least one request; some adapter has exactly 8 in every draw; the counts sum to 16.
All inputs are finite; a program needn't handle non-finite values.
Results may differ from the reference program's by a relative error of at most 0.022.
The reference program's roundings to bfloat16 on the way count: a program that leaves them out, or rounds other values in their place, can miss the bound.
Values may be sent and summed in bfloat16 or wider, within the bound.
A program may use at most 128 MiB of HBM per device.

```python
import math
import jax
import jax.numpy as jnp
from jax import lax

D = 7168
HEAD_COUNT = 128
NOPE_WIDTH = 128
ROPE_WIDTH = 64
VALUE_WIDTH = 128
LATENT_CHANNELS = 512
QUERY_CHANNELS = 1536
ADAPTER_RANK = 16
ADAPTER_COUNT = 8
STEPS = 2
REQ = 16
CAP = 8
CONTEXT = 32768


def adapter_groups(key):
    extra_rows = REQ - ADAPTER_COUNT
    key_order, key_room = jax.random.split(key)
    shuffled = jax.random.permutation(key_order, ADAPTER_COUNT)
    headroom = jax.random.randint(key_room, (ADAPTER_COUNT,), 1, CAP).astype(jnp.int32)
    headroom = headroom.at[0].set(CAP - 1)
    before_one = jnp.cumsum(headroom) - headroom
    first_pass = jnp.clip(extra_rows - before_one, 0, headroom)
    remaining = extra_rows - jnp.sum(first_pass)
    spare_room = CAP - 1 - first_pass
    before_two = jnp.cumsum(spare_room) - spare_room
    second_pass = jnp.clip(remaining - before_two, 0, spare_room)
    group_sizes = (1 + first_pass + second_pass).astype(jnp.int32)
    sizes_drawn = jnp.zeros((ADAPTER_COUNT,), jnp.int32).at[shuffled].set(group_sizes)
    starts = (jnp.cumsum(sizes_drawn) - sizes_drawn).astype(jnp.int32)
    return (sizes_drawn, starts)


def draw_group_request_count(key, part):
    sizes_drawn, starts = adapter_groups(key)
    return sizes_drawn


def draw_group_first_request(key, part):
    sizes_drawn, starts = adapter_groups(key)
    return starts


def draw_request_adapter(key, part):
    sizes_drawn, starts = adapter_groups(key)
    positions = jnp.arange(REQ, dtype=jnp.int32)
    below = (starts[None, :] <= positions[:, None]).astype(jnp.int32)
    return (jnp.sum(below, axis=1) - 1).astype(jnp.int32)


def draw_prefix_latent_cache(key, part):
    key = jax.random.fold_in(key, 7)
    key_main = jax.random.fold_in(key, 0)
    values = 2.5 * jnp.clip(jax.random.normal(key_main, (CONTEXT, LATENT_CHANNELS + ROPE_WIDTH), jnp.float32), -6.0, 6.0)
    return values.astype(jnp.bfloat16)


def draw_normed_query_latent(key, part):
    key = jax.random.fold_in(key, 11)
    key_main, key_scale, key_pick = jax.random.split(key, 3)
    entries = jnp.clip(jax.random.normal(key_main, (STEPS, REQ, QUERY_CHANNELS), jnp.float32), -6.0, 6.0)
    lowest = -0.6931472
    highest = 2.0794415
    log_scale = jax.random.uniform(key_scale, (REQ,), jnp.float32, lowest, highest)
    picked = jax.random.permutation(key_pick, REQ)
    log_scale = log_scale.at[picked[0]].set(highest).at[picked[1]].set(lowest)
    values = entries * jnp.exp(log_scale)[None, :, None]
    return values.astype(jnp.bfloat16)


def block_scale(stream_key, shape, cuts, low, largest):
    gain = 1.0
    for axis_at, shards_of in cuts:
        draws = jax.random.uniform(jax.random.fold_in(jax.random.fold_in(stream_key, 6), axis_at), (shards_of,), jnp.float32, low / len(cuts), largest / len(cuts))
        gain = gain * jnp.repeat(jnp.exp(draws), shape[axis_at] // shards_of).reshape((-1,) + (1,) * (len(shape) - 1 - axis_at))
    return gain


def noise(stream_key, shape, scale, reach, shards=(), kind=jnp.bfloat16):
    array = scale * jax.random.normal(stream_key, shape, jnp.float32)
    if shards:
        array = array * block_scale(stream_key, shape, shards, -0.22, 0.18)
    return jnp.clip(array, -reach, reach).astype(kind)


def setup_inputs(seed: int = 0) -> dict:
    key_list = jax.random.split(jax.random.key(seed), 17)
    normed_query_latent = draw_normed_query_latent(jax.random.fold_in(key_list[16], 71), 0)
    fresh_token_latent = noise(key_list[1], (STEPS, REQ, LATENT_CHANNELS + ROPE_WIDTH), 4.0, 16.0)
    prefix_latent_cache = draw_prefix_latent_cache(jax.random.fold_in(key_list[16], 71), 0)
    query_up_weight = noise(key_list[3], (QUERY_CHANNELS, HEAD_COUNT * (NOPE_WIDTH + ROPE_WIDTH)), QUERY_CHANNELS ** -0.5, 0.15625, ((1, 512),))
    key_up_weight = noise(key_list[4], (HEAD_COUNT, NOPE_WIDTH, LATENT_CHANNELS), NOPE_WIDTH ** -0.5, 0.5, ((0, 8), (2, 64)))
    value_up_weight = noise(key_list[5], (HEAD_COUNT, LATENT_CHANNELS, VALUE_WIDTH), LATENT_CHANNELS ** -0.5, 0.25, ((0, 8), (1, 64)))
    output_weight = noise(key_list[6], (HEAD_COUNT * VALUE_WIDTH, D), (HEAD_COUNT * VALUE_WIDTH) ** -0.5, 0.046875, ((0, 8), (1, 64)))
    adapter_query_down = noise(key_list[7], (ADAPTER_COUNT, QUERY_CHANNELS, ADAPTER_RANK), QUERY_CHANNELS ** -0.5, 0.15625)
    adapter_query_up = noise(key_list[8], (ADAPTER_COUNT, ADAPTER_RANK, HEAD_COUNT * (NOPE_WIDTH + ROPE_WIDTH)), ADAPTER_RANK ** -0.5, 1.5, ((2, 512),))
    adapter_key_down = noise(key_list[9], (ADAPTER_COUNT, LATENT_CHANNELS, ADAPTER_RANK), ADAPTER_RANK ** -0.5, 1.5, ((1, 64),))
    adapter_key_up = noise(key_list[10], (ADAPTER_COUNT, ADAPTER_RANK, HEAD_COUNT * NOPE_WIDTH), NOPE_WIDTH ** -0.5, 0.5, ((2, 8),))
    adapter_value_down = noise(key_list[11], (ADAPTER_COUNT, LATENT_CHANNELS, ADAPTER_RANK), LATENT_CHANNELS ** -0.5, 0.25, ((1, 64),))
    adapter_value_up = noise(key_list[12], (ADAPTER_COUNT, ADAPTER_RANK, HEAD_COUNT * VALUE_WIDTH), ADAPTER_RANK ** -0.5, 1.5, ((2, 8),))
    request_adapter = draw_request_adapter(jax.random.fold_in(key_list[16], 71), 0)
    group_first_request = draw_group_first_request(jax.random.fold_in(key_list[16], 71), 0)
    group_request_count = draw_group_request_count(jax.random.fold_in(key_list[16], 71), 0)
    return dict(normed_query_latent=normed_query_latent, fresh_token_latent=fresh_token_latent, prefix_latent_cache=prefix_latent_cache, query_up_weight=query_up_weight, key_up_weight=key_up_weight, value_up_weight=value_up_weight, output_weight=output_weight, adapter_query_down=adapter_query_down, adapter_query_up=adapter_query_up, adapter_key_down=adapter_key_down, adapter_key_up=adapter_key_up, adapter_value_down=adapter_value_down, adapter_value_up=adapter_value_up, request_adapter=request_adapter, group_first_request=group_first_request, group_request_count=group_request_count)


def rounded_wide(values):
    return lax.optimization_barrier(values.astype(jnp.bfloat16)).astype(jnp.float32)

def slot_places(request_adapter, group_first_request, group_request_count, capacity):
    adapter_list = group_first_request.shape[0]
    adapter_indicator = request_adapter[:, None] == jnp.arange(adapter_list, dtype=jnp.int32)[None, :]
    own_start = lax.optimization_barrier(jnp.sum(jnp.where(adapter_indicator, group_first_request[None, :], 0), axis=1)).astype(jnp.int32)
    own_count = lax.optimization_barrier(jnp.sum(jnp.where(adapter_indicator, group_request_count[None, :], 0), axis=1)).astype(jnp.int32)
    within = jnp.arange(request_adapter.shape[0], dtype=jnp.int32) - own_start
    is_live = jnp.logical_and(within >= 0, within < own_count)
    slot_index = (request_adapter * capacity + jnp.clip(within, 0, capacity - 1)).astype(jnp.int32)
    return (adapter_indicator, slot_index, is_live)

def padded_rows(values, group_first_request, capacity):
    steps_n = values.shape[0]
    padding_rows = jnp.zeros((steps_n, capacity) + values.shape[2:], values.dtype)
    extended = jnp.concatenate([values, padding_rows], axis=1)
    pick_rows = (group_first_request[:, None] + jnp.arange(capacity, dtype=jnp.int32)[None, :]).reshape(-1).astype(jnp.int32)
    gathered = jnp.take(extended, pick_rows, axis=1)
    return gathered.reshape((steps_n, group_first_request.shape[0], capacity) + values.shape[2:])

def back_to_requests(padded, slot_index, is_live):
    steps_n = padded.shape[0]
    merged_slots = padded.reshape((steps_n, -1) + padded.shape[3:])
    request_rows = jnp.take(merged_slots, slot_index, axis=1)
    live_mask = is_live.reshape((1, -1) + (1,) * (request_rows.ndim - 2))
    return jnp.where(live_mask, request_rows, jnp.zeros_like(request_rows))

def spread_rank(low_rank, adapter_indicator):
    adapter_list = adapter_indicator.shape[1]
    extra_dims = low_rank.ndim - 3
    mask_shape = (1, adapter_indicator.shape[0]) + (1,) * extra_dims + (adapter_list, 1)
    placed = jnp.where(adapter_indicator.reshape(mask_shape), low_rank[..., None, :], jnp.zeros((), low_rank.dtype))
    return placed.reshape(low_rank.shape[:-1] + (adapter_list * low_rank.shape[-1],))

def reference(normed_query_latent, fresh_token_latent, prefix_latent_cache, query_up_weight, key_up_weight, value_up_weight, output_weight, adapter_query_down, adapter_query_up, adapter_key_down, adapter_key_up, adapter_value_down, adapter_value_up, request_adapter, group_first_request, group_request_count):
    widened_rows = jnp.float32
    highest = lax.Precision.HIGHEST
    steps_n, request_n, _ = normed_query_latent.shape
    adapter_list = ADAPTER_COUNT
    capacity = CAP
    head_width = NOPE_WIDTH + ROPE_WIDTH
    adapter_indicator, slot_index, is_live = slot_places(request_adapter, group_first_request, group_request_count, capacity)
    latent_zero_fill = padded_rows(normed_query_latent, group_first_request, capacity)
    reduced_query = jnp.einsum('pmvx,mxe->pmve', latent_zero_fill.astype(widened_rows), adapter_query_down.astype(widened_rows)).astype(jnp.bfloat16)
    reduced_query = back_to_requests(reduced_query, slot_index, is_live)
    query_adapter_table = adapter_query_up.reshape(adapter_list * ADAPTER_RANK, -1).astype(widened_rows)
    query_base = jnp.einsum('srq,qc->src', normed_query_latent.astype(widened_rows), query_up_weight.astype(widened_rows))
    query_delta = jnp.einsum('srj,jc->src', spread_rank(reduced_query, adapter_indicator).astype(widened_rows), query_adapter_table)
    queries = (query_base + query_delta).astype(jnp.bfloat16).reshape(steps_n, request_n, HEAD_COUNT, head_width)
    query_unrotated = queries[..., :NOPE_WIDTH]
    query_pe = queries[..., NOPE_WIDTH:]
    nope_pad = padded_rows(query_unrotated, group_first_request, capacity)
    key_adapter_factor = adapter_key_up.reshape(adapter_list, ADAPTER_RANK, HEAD_COUNT, NOPE_WIDTH).astype(widened_rows)
    reduced_key = jnp.einsum('sachd,akhd->sachk', nope_pad.astype(widened_rows), key_adapter_factor).astype(jnp.bfloat16)
    reduced_key = back_to_requests(reduced_key, slot_index, is_live)
    key_adapter_table = jnp.transpose(adapter_key_down, (0, 2, 1)).reshape(adapter_list * ADAPTER_RANK, LATENT_CHANNELS).astype(widened_rows)
    latent_base = jnp.einsum('srhd,hdl->srhl', query_unrotated.astype(widened_rows), key_up_weight.astype(widened_rows))
    latent_delta = jnp.einsum('srhj,jl->srhl', spread_rank(reduced_key, adapter_indicator).astype(widened_rows), key_adapter_table)
    latent_queries = (latent_base + latent_delta).astype(jnp.bfloat16)
    cache_lat = prefix_latent_cache[:, :LATENT_CHANNELS].astype(widened_rows)
    cache_pe = prefix_latent_cache[:, LATENT_CHANNELS:].astype(widened_rows)
    new_lat = fresh_token_latent[..., :LATENT_CHANNELS].astype(widened_rows)
    new_pe = fresh_token_latent[..., LATENT_CHANNELS:].astype(widened_rows)
    down_factor_rows = jnp.take(adapter_value_down, request_adapter, axis=0).astype(widened_rows)
    score_scale = 1.0 / math.sqrt(head_width)
    step_ids = jnp.arange(steps_n, dtype=jnp.int32)
    causal = step_ids[None, :] <= step_ids[:, None]
    value_adapter_tables = jnp.transpose(adapter_value_up.reshape(adapter_list * ADAPTER_RANK, HEAD_COUNT, VALUE_WIDTH), (1, 0, 2))

    def one_head(inputs):
        lat_query, pe_query, value_up, value_adapter_table = inputs
        lat_query = lat_query.astype(widened_rows)
        pe_query = pe_query.astype(widened_rows)
        scores = (jnp.einsum('srl,jl->srj', lat_query, cache_lat) + jnp.einsum('sre,je->srj', pe_query, cache_pe)) * score_scale
        own_scores = (jnp.einsum('srl,trl->srt', lat_query, new_lat) + jnp.einsum('sre,tre->srt', pe_query, new_pe)) * score_scale
        own_scores = jnp.where(causal[:, None, :], own_scores, -jnp.inf)
        row_max = jnp.maximum(lax.optimization_barrier(jnp.max(scores, axis=2)), lax.optimization_barrier(jnp.max(own_scores, axis=2)))
        weights = jnp.exp(scores - row_max[..., None])
        own_weights = jnp.exp(own_scores - row_max[..., None])
        row_total = lax.optimization_barrier(jnp.sum(weights, axis=2)) + lax.optimization_barrier(jnp.sum(own_weights, axis=2))
        latent_sum = jnp.einsum('srj,jl->srl', rounded_wide(weights), cache_lat) + jnp.einsum('srt,trl->srl', rounded_wide(own_weights), new_lat)
        value_part = jnp.einsum('srl,lv->srv', latent_sum, value_up.astype(widened_rows), precision=highest) / row_total[..., None]
        low_value = jnp.einsum('srl,rlk->srk', latent_sum, down_factor_rows, precision=highest) / row_total[..., None]
        low_value = low_value.astype(jnp.bfloat16)
        value_delta = jnp.einsum('srj,jv->srv', spread_rank(low_value, adapter_indicator).astype(widened_rows), value_adapter_table.astype(widened_rows))
        return (value_part + value_delta).astype(jnp.bfloat16)
    latent_heads = jnp.transpose(latent_queries, (2, 0, 1, 3))
    pe_heads = jnp.transpose(query_pe, (2, 0, 1, 3))
    head_outputs = lax.map(one_head, (latent_heads, pe_heads, value_up_weight, value_adapter_tables))
    attention = jnp.transpose(head_outputs, (1, 2, 0, 3)).reshape(steps_n, request_n, HEAD_COUNT * VALUE_WIDTH)
    mixed = jnp.einsum('srf,fd->rsd', attention.astype(widened_rows), output_weight.astype(widened_rows))
    return mixed.astype(jnp.bfloat16)
```

```python
import functools
import math

import jax
import jax.numpy as jnp
from jax import lax
from jax.experimental import pallas as pl
from jax.experimental.pallas import tpu as pltpu
from jax.sharding import PartitionSpec as P

MESH = pl.DeviceIdType.MESH
F32 = jnp.float32
BF16 = jnp.bfloat16

CTX = 64
CHIPS = CTX // 2
GROUPS = 8
HEADS = 16
HALF = HEADS // 2
ROWS = 32
REQ = 16
NOPE = 128
ROPE = 64
LAT = 512
COLS = 48
KEYS = 512
WIDTH = 112
SCALE = 1.0 / math.sqrt(NOPE + ROPE)


def mm(a, b):
    return lax.dot_general(a, b, (((1,), (0,)), ((), ())), preferred_element_type=F32)


def mm_t(a, b):
    return lax.dot_general(a, b, (((1,), (1,)), ((), ())), preferred_element_type=F32)


def kernel(
    x_hbm,
    fresh_hbm,
    cache_hbm,
    wq_hbm,
    kup_hbm,
    vup_hbm,
    wo_hbm,
    aqd_hbm,
    aqu_hbm,
    akd_hbm,
    aku_hbm,
    avd_hbm,
    avu_hbm,
    adapter_s,
    first_s,
    count_s,
    out_ref,
    x_v,
    fresh_v,
    cache_v,
    wq_v,
    kup_v,
    vup_v,
    wo_v,
    aqd_v,
    aqu_v,
    akd_v,
    aku_v,
    avd_v,
    avu_v,
    kmsg,
    vmsg,
    kw,
    vw,
    qcol,
    lq_s,
    pe_s,
    lat,
    pos,
    acc_s,
    acc_r,
    ml_s,
    ml_r,
    turned,
    live_mask,
    own_mask,
    att,
    part,
    part_r,
    load_sem,
    send_sem,
    recv_sem,
):
    me = lax.axis_index("ctx")
    group = lax.axis_index("head")
    chip = me // 2
    core = me % 2
    head_up = me // 4
    quarter = me % 4
    up_core = head_up // HALF
    head_own = core * HALF + chip // 4
    block = chip % 4

    barrier = pltpu.get_barrier_semaphore()

    def greet(k, carry):
        pl.semaphore_signal(
            barrier, inc=1, device_id=((me + k) % CTX, group), device_id_type=MESH
        )
        return carry

    lax.fori_loop(1, CTX, greet, 0)

    def greet_group(k, carry):
        pl.semaphore_signal(
            barrier, inc=1, device_id=(me, (group + k) % GROUPS), device_id_type=MESH
        )
        return carry

    lax.fori_loop(1, GROUPS, greet_group, 0)

    up_col = pl.multiple_of(head_up * NOPE, NOPE)
    own_col = pl.multiple_of(head_own * NOPE, NOPE)
    loads = [
        pltpu.make_async_copy(src, dst, load_sem.at[n])
        for n, (src, dst) in enumerate(
            (
                (kup_hbm, kup_v),
                (akd_hbm, akd_v),
                (x_hbm, x_v),
                (aqd_hbm, aqd_v),
                (wq_hbm, wq_v),
                (aqu_hbm, aqu_v),
                (vup_hbm, vup_v),
                (avd_hbm, avd_v),
                (aku_hbm.at[:, pl.ds(up_col, NOPE)], aku_v),
                (cache_hbm, cache_v.at[0]),
                (fresh_hbm, fresh_v),
                (avu_hbm.at[:, pl.ds(own_col, NOPE)], avu_v),
                (wo_hbm, wo_v),
            )
        )
    ]
    for load in loads:
        load.start()
    (
        kup_l,
        akd_l,
        x_l,
        aqd_l,
        wq_l,
        aqu_l,
        vup_l,
        avd_l,
        aku_l,
        cache_l,
        fresh_l,
        avu_l,
        wo_l,
    ) = loads

    lane_adapter = lax.broadcasted_iota(jnp.int32, (ROWS, 128), 1) // 16
    row_request = lax.broadcasted_iota(jnp.int32, (ROWS, 128), 0) % REQ
    adapter = jnp.zeros((ROWS, 128), jnp.int32)
    first = jnp.zeros((ROWS, 128), jnp.int32)
    count = jnp.zeros((ROWS, 128), jnp.int32)
    for r in range(REQ):
        adapter = jnp.where(row_request == r, adapter_s[r], adapter)
    for a in range(8):
        first = jnp.where(lane_adapter == a, first_s[a], first)
        count = jnp.where(lane_adapter == a, count_s[a], count)
    owns = adapter == lane_adapter
    within = row_request - first
    live = jnp.logical_and(owns, jnp.logical_and(within >= 0, within < count))
    own_mask[...] = jnp.where(owns, 1.0, 0.0).astype(F32)
    live_mask[...] = jnp.where(live, 1.0, 0.0).astype(F32)

    kup_l.wait()
    akd_l.wait()
    table = jnp.concatenate([akd_v[a].astype(F32) for a in range(8)], axis=1)
    for h in range(HEADS):
        kmsg[h] = jnp.concatenate([kup_v[h].astype(F32), table], axis=0).astype(BF16)

    pl.semaphore_wait(barrier, CTX - 1 + GROUPS - 1)

    def send(src, dst, n, ctx, y):
        return pltpu.make_async_remote_copy(
            src_ref=src,
            dst_ref=dst,
            send_sem=send_sem.at[n],
            recv_sem=recv_sem.at[n],
            device_id=(ctx, y),
            device_id_type=MESH,
        )

    def arrived(ref, n):
        pltpu.make_async_copy(ref, ref, recv_sem.at[n]).wait()

    def sent(ref, n):
        pltpu.make_async_copy(ref, ref, send_sem.at[n]).wait()

    def send_or_keep(src, dst, n, ctx):
        @pl.when(ctx == me)
        def _():
            pltpu.make_async_copy(src, dst, recv_sem.at[n]).start()

        @pl.when(ctx != me)
        def _():
            send(src, dst, n, ctx, group).start()

    def send_keys(k, carry):
        h = (head_up + k) % HEADS
        send_or_keep(kmsg.at[h], kw.at[me % 16], 0, 4 * h + me // 16)
        return carry

    lax.fori_loop(0, HEADS, send_keys, 0)

    sibling = 2 * chip + 1 - core
    share = send(cache_hbm, cache_v.at[1], 1, sibling, group)
    share.start()

    x_l.wait()
    aqd_l.wait()
    x = x_v[...]
    low = (mm_t(x, aqd_v[...]) * live_mask[...]).astype(BF16)
    wq_l.wait()
    aqu_l.wait()
    cols = (mm_t(x, wq_v[...]) + mm(low, aqu_v[...])).astype(BF16)
    qcol[quarter] = jnp.concatenate(
        [cols.astype(F32), jnp.zeros((ROWS, 128 - COLS), F32)], axis=1
    ).astype(BF16)

    for k in range(1, 4):
        send(
            qcol.at[quarter],
            qcol.at[quarter],
            2,
            4 * head_up + (quarter + k) % 4,
            group,
        ).start()

    vup_l.wait()
    avd_l.wait()
    table = jnp.concatenate([avd_v[a].astype(F32) for a in range(8)], axis=1)
    for h in range(HEADS):
        vmsg[h] = jnp.concatenate([vup_v[h].astype(F32), table], axis=0).astype(BF16)

    def send_values(k, carry):
        dest = (me + k) % CTX
        h = HALF * (dest % 2) + dest // 8
        send_or_keep(vmsg.at[h], vw.at[me], 3, dest)
        return carry

    arrived(qcol.at[pl.ds(0, 3)], 2)
    q0 = qcol[0].astype(F32)
    q1 = qcol[1].astype(F32)
    q2 = qcol[2].astype(F32)
    q3 = qcol[3].astype(F32)
    nope = jnp.concatenate([q0[:, :48], q1[:, :48], q2[:, :32]], axis=1).astype(BF16)
    pe = jnp.concatenate([q2[:, 32:48], q3[:, :48]], axis=1)
    pe_s[...] = jnp.concatenate([pe[:16], pe[16:]], axis=1).astype(BF16)

    def send_pe(k, carry):
        there = 4 * ((chip // 4 + k) % 8) + quarter
        send_or_keep(pe_s, pos.at[head_up % HALF], 4, 2 * there + up_core)
        return carry

    lax.fori_loop(0, 8, send_pe, 0)

    aku_l.wait()
    low_key = (mm_t(nope, aku_v[...]) * live_mask[...]).astype(BF16)
    arrived(kw, 0)
    kwf = kw[...].astype(F32)
    key_up = kwf[:, :8].reshape(128, 128).astype(BF16)
    key_down = kwf[:, 8:].reshape(128, 128).astype(BF16)
    lq_s[...] = (mm_t(nope, key_up) + mm_t(low_key, key_down)).astype(BF16)

    slot = (head_up % HALF) * 4 + quarter

    def send_lat(k, carry):
        there = (chip + k) % CHIPS
        send_or_keep(lq_s, lat.at[slot], 5, 2 * there + up_core)
        return carry

    lax.fori_loop(0, CHIPS, send_lat, 0)
    lax.fori_loop(0, CTX, send_values, 0)

    arrived(pos, 4)
    arrived(lat, 5)
    q_lat = jnp.concatenate(
        [
            jnp.concatenate([lat[4 * h + j] for j in range(4)], axis=1)
            for h in range(HALF)
        ],
        axis=0,
    )
    both = pos[...].astype(F32)
    q_pe = (
        jnp.concatenate([both[:, :, :ROPE], both[:, :, ROPE:]], axis=1)
        .reshape(HALF * ROWS, ROPE)
        .astype(BF16)
    )
    cache_l.wait()
    share.wait_recv()
    scores = [
        (mm(q_lat, cache_v[n, :LAT]) + mm(q_pe, cache_v[n, LAT:])) * SCALE
        for n in range(2)
    ]
    top = jnp.maximum(
        jnp.max(scores[0], axis=1, keepdims=True),
        jnp.max(scores[1], axis=1, keepdims=True),
    )
    weights = [jnp.exp(s - top) for s in scores]
    total = jnp.sum(weights[0], axis=1, keepdims=True) + jnp.sum(
        weights[1], axis=1, keepdims=True
    )
    lane = lax.broadcasted_iota(jnp.int32, (HALF * ROWS, 128), 1)
    stats = jnp.where(lane == 0, top, jnp.where(lane == 1, total, 0.0))
    stats = stats.T
    for half in range(2):
        ml_s[half] = stats[0:2, 128 * half : 128 * half + 128]

    def send_stats(k, carry):
        there = (chip + k) % CHIPS
        send(ml_s.at[there // 16], ml_r.at[chip], 6, 2 * there + core, group).start()
        return carry

    lax.fori_loop(1, CHIPS, send_stats, 0)
    pltpu.make_async_copy(ml_s.at[chip // 16], ml_r.at[chip], recv_sem.at[6]).start()

    summed = sum(
        mm_t(weights[n].astype(BF16), cache_v[n, :LAT]) for n in range(2)
    )
    for pair in range(2):
        low_half = summed[:, 256 * pair : 256 * pair + 128].reshape(CHIPS, 8, 128)
        high_half = summed[:, 256 * pair + 128 : 256 * pair + 256].reshape(
            CHIPS, 8, 128
        )
        acc_s[:, 16 * pair : 16 * pair + 16] = jnp.concatenate(
            [low_half, high_half], axis=1
        ).astype(BF16)

    def send_acc(k, carry):
        there = (chip + k) % CHIPS
        send(acc_s.at[there], acc_r.at[chip], 7, 2 * there + core, group).start()
        return carry

    lax.fori_loop(1, CHIPS, send_acc, 0)
    pltpu.make_async_copy(acc_s.at[chip], acc_r.at[chip], recv_sem.at[7]).start()

    fresh_l.wait()
    fresh = fresh_v[...]
    own_head = (chip // 4) * 4
    own_lat = jnp.concatenate([lat[own_head + j] for j in range(4)], axis=1)
    both = pos[chip // 4].astype(F32)
    own_pe = jnp.concatenate([both[:, :ROPE], both[:, ROPE:]], axis=0).astype(BF16)
    own_scores = (mm_t(own_lat, fresh[:, :LAT]) + mm_t(own_pe, fresh[:, LAT:])) * SCALE
    row = lax.broadcasted_iota(jnp.int32, (ROWS, ROWS), 0)
    key = lax.broadcasted_iota(jnp.int32, (ROWS, ROWS), 1)
    seen = jnp.logical_and(row % REQ == key % REQ, key // REQ <= row // REQ)
    own_scores = jnp.where(seen, own_scores, -jnp.inf)
    own_top = jnp.max(own_scores, axis=1, keepdims=True)
    own_weights = jnp.exp(own_scores - own_top)
    own_total = jnp.sum(own_weights, axis=1, keepdims=True)
    own_sum = mm(own_weights.astype(BF16), fresh[:, :LAT])

    def mine(a):
        rows = [a[8 * b : 8 * b + 8] for b in range(4)]
        low_pair = jnp.where(block == 0, rows[0], rows[1])
        high_pair = jnp.where(block == 2, rows[2], rows[3])
        return jnp.where(block < 2, low_pair, high_pair)

    own_top = mine(own_top)
    own_total = mine(own_total)
    own_sum = mine(own_sum)
    mask = mine(own_mask[...])

    arrived(vw, 3)
    vwf = vw[...].astype(F32)
    value_up = vwf[:, :8].reshape(LAT, 128).astype(BF16)
    value_down = vwf[:, 8:].reshape(LAT, 128).astype(BF16)

    arrived(ml_r, 6)
    ml = ml_r[...]
    turned[...] = jnp.concatenate(
        [ml[:, 0], ml[:, 1], jnp.zeros((64, 128), F32)], axis=0
    ).T
    stats = turned[pl.ds(pl.multiple_of(8 * (chip % 16), 8), 8), :]
    tops = stats[:, :CHIPS]
    totals = stats[:, CHIPS : 2 * CHIPS]
    joined = jnp.maximum(jnp.max(tops, axis=1, keepdims=True), own_top)
    factors = jnp.exp(tops - joined)
    own_factor = jnp.exp(own_top - joined)
    row_total = (
        jnp.sum(factors * totals, axis=1, keepdims=True) + own_factor * own_total
    )
    arrived(acc_r, 7)
    latent = own_sum * own_factor
    latent = [latent[:, 128 * j : 128 * j + 128] for j in range(4)]
    for n in range(CHIPS):
        factor = factors[:, n : n + 1]
        got = acc_r[n].astype(F32)
        for j in range(4):
            latent[j] = latent[j] + factor * got[8 * j : 8 * j + 8]
    latent = jnp.concatenate(latent, axis=1) / row_total

    high = latent.astype(BF16).astype(F32)
    rest = latent - high
    middle = rest.astype(BF16).astype(F32)
    parts = jnp.concatenate([high, middle, rest - middle], axis=0).astype(BF16)
    value = mm(parts, value_up)
    low_value = mm(parts, value_down)
    value = value[0:8] + value[8:16] + value[16:24]
    low_value = low_value[0:8] + low_value[8:16] + low_value[16:24]
    low_value = (low_value * mask).astype(BF16)
    avu_l.wait()
    att[core * CHIPS + chip] = (value + mm(low_value, avu_v[...])).astype(BF16)

    place = core * CHIPS + chip

    def send_att(k, carry):
        send(att.at[place], att.at[place], 8, (me + k) % CTX, group).start()
        return carry

    lax.fori_loop(1, CTX, send_att, 0)
    wo_l.wait()
    arrived(att.at[pl.ds(0, CTX - 1)], 8)
    rows = att[...].astype(F32)
    rows = jnp.concatenate(
        [rows[4 * h : 4 * h + 4].reshape(ROWS, 128) for h in range(HEADS)], axis=1
    ).astype(BF16)
    mixed = mm_t(rows, wo_v[...])
    mixed = jnp.concatenate([mixed, jnp.zeros((ROWS, 128 - WIDTH), F32)], axis=1)
    for y in range(GROUPS):
        part[y] = jnp.concatenate(
            [mixed[2 * y : 2 * y + 2], mixed[REQ + 2 * y : REQ + 2 * y + 2]], axis=0
        )

    def send_part(k, carry):
        there = (group + k) % GROUPS
        send(part.at[there], part_r.at[group], 9, me, there).start()
        return carry

    lax.fori_loop(1, GROUPS, send_part, 0)
    part_r[group] = part[group]
    arrived(part_r.at[pl.ds(0, GROUPS - 1)], 9)
    done = part_r[0]
    for y in range(1, GROUPS):
        done = done + part_r[y]
    out_ref[...] = done

    keeps_key = jnp.logical_and(me // 4 == head_up, me % 4 == me // 16)

    @pl.when(keeps_key)
    def _():
        sent(kw.at[pl.ds(0, 15)], 0)

    @pl.when(jnp.logical_not(keeps_key))
    def _():
        sent(kw, 0)

    share.wait_send()
    sent(qcol.at[pl.ds(0, 3)], 2)
    sent(vw.at[pl.ds(0, CTX - 1)], 3)
    keeps_pe = jnp.logical_and(core == up_core, chip % 4 == quarter)

    @pl.when(keeps_pe)
    def _():
        sent(pos.at[pl.ds(0, 7)], 4)

    @pl.when(jnp.logical_not(keeps_pe))
    def _():
        sent(pos, 4)

    @pl.when(core == up_core)
    def _():
        sent(lat.at[pl.ds(0, CHIPS - 1)], 5)

    @pl.when(core != up_core)
    def _():
        sent(lat, 5)

    sent(ml_r.at[pl.ds(0, CHIPS - 1)], 6)
    sent(acc_r.at[pl.ds(0, CHIPS - 1)], 7)
    sent(att.at[pl.ds(0, CTX - 1)], 8)
    sent(part_r.at[pl.ds(0, GROUPS - 1)], 9)


def body(
    normed_query_latent,
    fresh_token_latent,
    prefix_latent_cache,
    query_up_weight,
    key_up_weight,
    value_up_weight,
    output_weight,
    adapter_query_down,
    adapter_query_up,
    adapter_key_down,
    adapter_key_up,
    adapter_value_down,
    adapter_value_up,
    request_adapter,
    group_first_request,
    group_request_count,
):
    operands = (
        normed_query_latent.reshape(ROWS, -1),
        fresh_token_latent.reshape(ROWS, -1),
        prefix_latent_cache.T,
        query_up_weight.T,
        jnp.transpose(key_up_weight, (0, 2, 1)),
        value_up_weight,
        output_weight.T,
        jnp.transpose(adapter_query_down, (0, 2, 1)).reshape(128, -1),
        adapter_query_up.reshape(128, COLS),
        adapter_key_down,
        adapter_key_up.reshape(128, -1),
        adapter_value_down,
        adapter_value_up.reshape(128, -1),
    )
    vmem = pltpu.VMEM
    done = pl.pallas_call(
        kernel,
        out_shape=jax.ShapeDtypeStruct((4, 128), F32),
        in_specs=[pl.BlockSpec(memory_space=pltpu.HBM)] * 13
        + [pl.BlockSpec(memory_space=pltpu.SMEM)] * 3,
        out_specs=pl.BlockSpec(memory_space=pltpu.VMEM),
        scratch_shapes=[
            vmem((ROWS, 1536), BF16),
            vmem((ROWS, LAT + ROPE), BF16),
            vmem((2, LAT + ROPE, KEYS), BF16),
            vmem((COLS, 1536), BF16),
            vmem((HEADS, 8, 128), BF16),
            vmem((HEADS, 8, 128), BF16),
            vmem((WIDTH, HEADS * 128), BF16),
            vmem((128, 1536), BF16),
            vmem((128, COLS), BF16),
            vmem((8, 8, 16), BF16),
            vmem((128, 128), BF16),
            vmem((8, 8, 16), BF16),
            vmem((128, 128), BF16),
            vmem((HEADS, 16, 128), BF16),
            vmem((HEADS, 16, 128), BF16),
            vmem((16, 16, 128), BF16),
            vmem((CTX, 16, 128), BF16),
            vmem((4, ROWS, 128), BF16),
            vmem((ROWS, 128), BF16),
            vmem((16, 128), BF16),
            vmem((CHIPS, ROWS, 128), BF16),
            vmem((HALF, 16, 128), BF16),
            vmem((CHIPS, ROWS, 128), BF16),
            vmem((CHIPS, ROWS, 128), BF16),
            vmem((2, 2, 128), F32),
            vmem((CHIPS, 2, 128), F32),
            vmem((128, 128), F32),
            vmem((ROWS, 128), F32),
            vmem((ROWS, 128), F32),
            vmem((CTX, 8, 128), BF16),
            vmem((GROUPS, 4, 128), F32),
            vmem((GROUPS, 4, 128), F32),
            pltpu.SemaphoreType.DMA((13,)),
            pltpu.SemaphoreType.DMA((10,)),
            pltpu.SemaphoreType.DMA((10,)),
        ],
        compiler_params=pltpu.CompilerParams(
            collective_id=0, has_side_effects=True, vmem_limit_bytes=48 * 2**20
        ),
        name="latent_attention",
    )(*operands, request_adapter, group_first_request, group_request_count)
    done = done[:, :WIDTH].reshape(2, 2, WIDTH)
    return jnp.transpose(done, (1, 0, 2)).astype(BF16)


def solution(mesh):
    placed = (
        P(),
        P(),
        P("ctx", None),
        P(None, ("head", "ctx")),
        P("head", None, "ctx"),
        P("head", "ctx", None),
        P("head", "ctx"),
        P(),
        P(None, None, ("head", "ctx")),
        P(None, "ctx", None),
        P(None, None, "head"),
        P(None, "ctx", None),
        P(None, None, "head"),
        P(),
        P(),
        P(),
    )
    return jax.shard_map(
        body, mesh=mesh, in_specs=placed, out_specs=P("head", None, "ctx"), check_vma=False
    )
```

```python
import functools
import math

import jax
import jax.numpy as jnp
from jax import lax
from jax.experimental import pallas as pl
from jax.experimental.pallas import tpu as pltpu
from jax.sharding import PartitionSpec as P

MESH = pl.DeviceIdType.MESH
F32 = jnp.float32
BF16 = jnp.bfloat16

CTX = 64
CHIPS = CTX // 2
GROUPS = 8
HEADS = 16
HALF = HEADS // 2
ROWS = 32
REQ = 16
NOPE = 128
ROPE = 64
LAT = 512
COLS = 48
KEYS = 512
WIDTH = 112
SCALE = 1.0 / math.sqrt(NOPE + ROPE)


def mm(a, b):
    return lax.dot_general(a, b, (((1,), (0,)), ((), ())), preferred_element_type=F32)


def mm_t(a, b):
    return lax.dot_general(a, b, (((1,), (1,)), ((), ())), preferred_element_type=F32)


def far_first(i, size):
    return size // 2 + ((i + 1) >> 1) * (1 - 2 * (i & 1))


def kernel(
    x_hbm,
    fresh_hbm,
    cache_hbm,
    wq_hbm,
    kup_hbm,
    vup_hbm,
    wo_hbm,
    aqd_hbm,
    aqu_hbm,
    akd_hbm,
    aku_hbm,
    avd_hbm,
    avu_hbm,
    adapter_s,
    first_s,
    count_s,
    out_ref,
    x_v,
    fresh_v,
    cache_v,
    wq_v,
    kup_v,
    vup_v,
    wo_v,
    aqd_v,
    aqu_v,
    akd_v,
    aku_v,
    avd_v,
    avu_v,
    kmsg,
    vmsg,
    kw,
    vw,
    col_s,
    qcol,
    lq_s,
    pe_s,
    lat,
    pos,
    acc_s,
    acc_r,
    ml_s,
    ml_r,
    turned,
    att,
    part,
    part_r,
    ready,
    load_sem,
    send_sem,
    recv_sem,
):
    me = lax.axis_index("ctx")
    group = lax.axis_index("head")
    chip = me >> 1
    core = me & 1
    x_at = me >> 4
    z_at = chip & 7
    place = me & 15
    head_made = me >> 2
    piece = me & 3
    head_up = 4 * (place & 3) + (place >> 2)
    up_core = head_up >> 3
    head_own = (chip ^ 4) >> 1
    block_own = (chip & 15) ^ 4
    step_own = chip & 1
    owner = core == chip >> 4

    def chip_at(i):
        dz = far_first(i >> 2, 8)
        dx = far_first(i & 3, 4)
        return (((x_at + dx) & 3) << 3) | ((z_at + dz) & 7)

    def group_of(z_there, pair):
        step = (pair - (z_there >> 1)) & 3
        near = jnp.logical_or(step == 0, step == 3 - 2 * (z_there & 1))
        return jnp.where(near, 0, 1)

    barrier = pltpu.get_barrier_semaphore()

    def greet(ctx, y):
        pl.semaphore_signal(barrier, inc=1, device_id=(ctx, y), device_id_type=MESH)

    def greet_plane(i, carry):
        z = (z_at + far_first(i, 8)) & 7
        greet(16 * x_at + 2 * z + core, group)
        greet(16 * x_at + 2 * z + 1 - core, group)
        return carry

    lax.fori_loop(0, 7, greet_plane, 0)
    line = [16 * ((x_at + d) & 3) + place for d in (2, 1, 3)]
    for ctx in line:
        greet(ctx, group)

    @pl.when(head_up >> 2 != x_at)
    def _():
        for n in range(4):
            greet(4 * head_up + n, group)

    def greet_group(i, carry):
        y = (group + far_first(i, GROUPS)) & (GROUPS - 1)
        greet(me, y)
        greet(me ^ 1, y)
        return carry

    lax.fori_loop(0, GROUPS - 1, greet_group, 0)
    greet(me ^ 1, group)

    up_col = pl.multiple_of(head_up * NOPE, NOPE)
    own_col = pl.multiple_of(head_own * NOPE, NOPE)
    half_col = pl.multiple_of(core * (HALF * NOPE), HALF * NOPE)
    other_col = pl.multiple_of((1 - core) * (HALF * NOPE), HALF * NOPE)
    pending = {}
    for n, (name, src, dst) in enumerate(
        (
            ("x", x_hbm, x_v),
            ("aqd", aqd_hbm, aqd_v),
            ("wq", wq_hbm, wq_v),
            ("aqu", aqu_hbm, aqu_v),
            ("kup", kup_hbm, kup_v),
            ("akd", akd_hbm, akd_v),
            ("vup", vup_hbm, vup_v),
            ("avd", avd_hbm, avd_v),
            ("aku", aku_hbm.at[:, pl.ds(up_col, NOPE)], aku_v),
            ("cache", cache_hbm, cache_v.at[0]),
            ("fresh", fresh_hbm, fresh_v),
            ("avu", avu_hbm.at[:, pl.ds(own_col, NOPE)], avu_v),
            ("wo", wo_hbm.at[:, pl.ds(half_col, HALF * NOPE)], wo_v.at[0]),
        )
    ):
        load = pltpu.make_async_copy(src, dst, load_sem.at[n])
        load.start()
        pending[name] = load.wait

    def wait(*names):
        for name in names:
            pending.pop(name)()

    def finish():
        wait(*list(pending))

    def send(src, dst, n, ctx, y, out=None):
        return pltpu.make_async_remote_copy(
            src_ref=src,
            dst_ref=dst,
            send_sem=send_sem.at[n if out is None else out],
            recv_sem=recv_sem.at[n],
            device_id=(ctx, y),
            device_id_type=MESH,
        )

    def send_or_keep(src, dst, n, ctx, y=None, out=None):
        y = group if y is None else y
        here = jnp.logical_and(ctx == me, y == group)

        @pl.when(here)
        def _():
            pltpu.make_async_copy(src, dst, recv_sem.at[n]).start()

        @pl.when(jnp.logical_not(here))
        def _():
            send(src, dst, n, ctx, y, out).start()

    def arrives(name, ref, n, when=None):
        wait_all = pltpu.make_async_copy(ref, ref, recv_sem.at[n]).wait
        pending[name] = wait_all if when is None else lambda: pl.when(when)(wait_all)

    def leaves(name, ref, n, kept=None, fewer=None):
        wait_all = pltpu.make_async_copy(ref, ref, send_sem.at[n]).wait

        def either():
            pl.when(kept)(pltpu.make_async_copy(fewer, fewer, send_sem.at[n]).wait)
            pl.when(jnp.logical_not(kept))(wait_all)

        pending[name] = wait_all if kept is None else either

    lane_adapter = lax.broadcasted_iota(jnp.int32, (REQ, 128), 1) // 16
    request = lax.broadcasted_iota(jnp.int32, (REQ, 128), 0)
    adapter = jnp.zeros((REQ, 128), jnp.int32)
    first = jnp.zeros((REQ, 128), jnp.int32)
    count = jnp.zeros((REQ, 128), jnp.int32)
    for r in range(REQ):
        adapter = jnp.where(request == r, adapter_s[r], adapter)
    for a in range(8):
        first = jnp.where(lane_adapter == a, first_s[a], first)
        count = jnp.where(lane_adapter == a, count_s[a], count)
    owns = adapter == lane_adapter
    within = request - first
    live = jnp.logical_and(owns, jnp.logical_and(within >= 0, within < count))
    own_mask = jnp.where(owns, 1.0, 0.0).astype(F32)
    live_mask = jnp.where(live, 1.0, 0.0).astype(F32)
    live_mask = jnp.concatenate([live_mask, live_mask], axis=0)

    wait("x", "aqd")
    x = x_v[...]
    low = (mm_t(x, aqd_v[...]) * live_mask).astype(BF16)
    wait("wq", "aqu")
    cols = (mm_t(x, wq_v[...]) + mm(low, aqu_v[...])).astype(BF16)
    col_s[...] = jnp.concatenate(
        [cols.astype(F32), jnp.zeros((ROWS, 128 - COLS), F32)], axis=1
    ).astype(BF16)

    wait("kup", "akd")
    table = jnp.concatenate([akd_v[a].astype(F32) for a in range(8)], axis=1)
    for h in range(HEADS):
        kmsg[h] = jnp.concatenate([kup_v[h].astype(F32), table], axis=0).astype(BF16)
    wait("vup", "avd")
    table = jnp.concatenate([avd_v[a].astype(F32) for a in range(8)], axis=1)
    for h in range(HEADS):
        vmsg[h] = jnp.concatenate([vup_v[h].astype(F32), table], axis=0).astype(BF16)

    pl.semaphore_wait(barrier, 15 + 3 + 3 + 2 * (GROUPS - 1))
    for ctx in line:
        pl.semaphore_signal(ready, inc=1, device_id=(ctx, group), device_id_type=MESH)
    pending["ready"] = lambda: pl.semaphore_wait(ready, 3)

    def send_keys(i, carry):
        z = (z_at + far_first(i, 8)) & 7
        for c in range(2):
            to = 2 * z + c
            send_or_keep(
                kmsg.at[4 * (to & 3) + (to >> 2)], kw.at[place], 0, 16 * x_at + to
            )
        return carry

    lax.fori_loop(0, 8, send_keys, 0)
    arrives("kw", kw, 0)
    leaves("kw out", kw.at[pl.ds(0, 15)], 0)

    to = ((head_made & 3) << 2) | (head_made >> 2)
    for i in range(4):
        send_or_keep(
            col_s, qcol.at[piece], 2, 16 * ((x_at + (2, 1, 3, 0)[i]) & 3) + to
        )
    arrives("qcol", qcol, 2)
    leaves("qcol out", qcol, 2, piece == x_at, qcol.at[pl.ds(0, 3)])

    wait("qcol")
    q0 = qcol[0].astype(F32)
    q1 = qcol[1].astype(F32)
    q2 = qcol[2].astype(F32)
    q3 = qcol[3].astype(F32)
    nope = jnp.concatenate([q0[:, :48], q1[:, :48], q2[:, :32]], axis=1).astype(BF16)
    pe = jnp.concatenate([q2[:, 32:48], q3[:, :48]], axis=1)
    pe_s[...] = jnp.concatenate([pe[:16], pe[16:]], axis=1).astype(BF16)

    wait("ready")

    def send_pe(i, carry):
        z = (z_at + far_first(i, 8)) & 7
        n = 4 + 8 * group_of(z, z_at >> 1)
        send_or_keep(
            pe_s, pos.at[head_up & 7], n, 16 * x_at + 2 * z + up_core, out=4
        )
        return carry

    lax.fori_loop(0, 8, send_pe, 0)
    half_pos = pos.at[pl.ds(0, HALF // 2)]
    arrives("pos 0", half_pos, 4)
    arrives("pos 1", half_pos, 12)
    leaves("pos out", pos, 4, core == up_core, pos.at[pl.ds(0, 7)])

    wait("aku")
    low_key = (mm_t(nope, aku_v[...]) * live_mask).astype(BF16)
    wait("kw")
    kwf = kw[...].astype(F32)
    key_up = kwf[:, :8].reshape(128, 128).astype(BF16)
    key_down = kwf[:, 8:].reshape(128, 128).astype(BF16)
    lq_s[...] = (mm_t(nope, key_up) + mm_t(low_key, key_down)).astype(BF16)

    slot = (head_up & 7) * 4 + x_at

    def send_lat(i, carry):
        there = chip_at(i)
        n = 5 + 6 * group_of(there & 7, z_at >> 1)
        send_or_keep(lq_s, lat.at[slot], n, 2 * there + up_core, out=5)
        return carry

    lax.fori_loop(0, CHIPS, send_lat, 0)
    leaves("lat out", lat, 5, core == up_core, lat.at[pl.ds(0, CHIPS - 1)])
    half_lat = lat.at[pl.ds(0, CHIPS // 2)]
    arrives("lat 0", half_lat, 5)
    arrives("lat 1", half_lat, 11)

    share = send(cache_hbm, cache_v.at[1], 1, me ^ 1, group)
    share.start()
    pending["share"] = share.wait_recv
    pending["share out"] = share.wait_send
    share = send(
        wo_hbm.at[:, pl.ds(other_col, HALF * NOPE)], wo_v.at[1], 10, me ^ 1, group
    )
    share.start()
    pending["wo share"] = share.wait_recv
    pending["wo share out"] = share.wait_send

    def send_values(i, carry):
        there = chip_at(i)
        send_or_keep(vmsg.at[(there ^ 4) >> 1], vw.at[me], 3, 2 * there + (there >> 4))
        return carry

    lax.fori_loop(0, CHIPS, send_values, 0)
    arrives("vw", vw, 3, owner)
    leaves(
        "vw out", vw.at[pl.ds(0, CHIPS)], 3, owner, vw.at[pl.ds(0, CHIPS - 1)]
    )

    next_pair = 2 * (z_at & 1) - 1
    pairs = [((z_at >> 1) + d) & 3 for d in (0, next_pair, 2, -next_pair)]

    def owner_of(block):
        return 2 * (16 * core + (block ^ 4)) + core

    for half in range(2):
        heads = [pairs[2 * half + (n >> 1)] + 4 * (n & 1) for n in range(4)]
        wait("pos %d" % half, "lat %d" % half)
        q_lat = jnp.concatenate(
            [
                jnp.concatenate([lat[4 * h + j] for j in range(4)], axis=1)
                for h in heads
            ],
            axis=0,
        )
        q_pe = []
        for h in heads:
            both = pos[h].astype(F32)
            q_pe += [both[:, :ROPE], both[:, ROPE:]]
        q_pe = jnp.concatenate(q_pe, axis=0).astype(BF16)
        if half == 0:
            wait("cache", "share")
        scores = [
            (mm(q_lat, cache_v[n, :LAT]) + mm(q_pe, cache_v[n, LAT:])) * SCALE
            for n in range(2)
        ]
        top = jnp.maximum(
            jnp.max(scores[0], axis=1, keepdims=True),
            jnp.max(scores[1], axis=1, keepdims=True),
        )
        weights = [jnp.exp(s - top) for s in scores]
        total = jnp.sum(weights[0], axis=1, keepdims=True) + jnp.sum(
            weights[1], axis=1, keepdims=True
        )
        lane = lax.broadcasted_iota(jnp.int32, (128, 128), 1)
        stats = jnp.where(lane == 0, top, jnp.where(lane == 1, total, 0.0)).T[:2]
        for n, h in enumerate(heads):
            ml_s[h] = stats if n == 0 else pltpu.roll(stats, 128 - 32 * n, 1)

        for h in heads:
            for step in range(2):
                send_or_keep(ml_s.at[h], ml_r.at[chip], 6, owner_of(2 * h + step))

        summed = sum(mm_t(weights[n].astype(BF16), cache_v[n, :LAT]) for n in range(2))
        for n, h in enumerate(heads):
            for step in range(2):
                rows = summed[32 * n + 16 * step : 32 * n + 16 * step + 16]
                for j in range(4):
                    acc_s[2 * h + step, 16 * j : 16 * j + 16] = rows[
                        :, 128 * j : 128 * j + 128
                    ].astype(BF16)

        for h in heads:
            for step in range(2):
                block = 2 * h + step
                send_or_keep(acc_s.at[block], acc_r.at[chip], 7, owner_of(block))

    arrives("ml", ml_r, 6, owner)
    leaves("ml out", ml_r.at[pl.ds(0, 16)], 6, owner, ml_r.at[pl.ds(0, 15)])
    arrives("acc", acc_r, 7, owner)
    leaves("acc out", acc_r.at[pl.ds(0, 16)], 7, owner, acc_r.at[pl.ds(0, 15)])

    wait("fresh", "avu")
    for name in ("vw", "ml", "acc"):
        pending.pop(name)

    def arrived(ref, n):
        pltpu.make_async_copy(ref, ref, recv_sem.at[n]).wait()

    @pl.when(owner)
    def _():
        fresh = fresh_v[...]
        own = head_own & 7
        own_rows = pl.ds(pl.multiple_of(REQ * step_own, REQ), REQ)
        own_lat = jnp.concatenate([lat[4 * own + j, own_rows] for j in range(4)], axis=1)
        both = pos[own].astype(F32)
        own_pe = jnp.where(step_own == 0, both[:, :ROPE], both[:, ROPE:]).astype(BF16)
        own_scores = (
            mm_t(own_lat, fresh[:, :LAT]) + mm_t(own_pe, fresh[:, LAT:])
        ) * SCALE
        row = lax.broadcasted_iota(jnp.int32, (REQ, ROWS), 0)
        key = lax.broadcasted_iota(jnp.int32, (REQ, ROWS), 1)
        seen = jnp.logical_and(row == key % REQ, key // REQ <= step_own)
        own_scores = jnp.where(seen, own_scores, -jnp.inf)
        own_top = jnp.max(own_scores, axis=1, keepdims=True)
        own_weights = jnp.exp(own_scores - own_top)
        own_total = jnp.sum(own_weights, axis=1, keepdims=True)
        own_sum = mm(own_weights.astype(BF16), fresh[:, :LAT])

        arrived(vw, 3)
        vwf = vw[...].astype(F32)
        value_up = vwf[:, :8].reshape(LAT, 128).astype(BF16)
        value_down = vwf[:, 8:].reshape(LAT, 128).astype(BF16)

        arrived(ml_r, 6)
        ml = ml_r[...]
        turned[...] = jnp.concatenate(
            [ml[:, 0], ml[:, 1], jnp.zeros((64, 128), F32)], axis=0
        ).T
        stats = turned[pl.ds(pl.multiple_of(REQ * step_own, REQ), REQ), :]
        tops = stats[:, :CHIPS]
        totals = stats[:, CHIPS : 2 * CHIPS]
        joined = jnp.maximum(jnp.max(tops, axis=1, keepdims=True), own_top)
        factors = jnp.exp(tops - joined)
        own_factor = jnp.exp(own_top - joined)
        row_total = (
            jnp.sum(factors * totals, axis=1, keepdims=True) + own_factor * own_total
        )
        latent = own_sum * own_factor
        latent = [latent[:, 128 * j : 128 * j + 128] for j in range(4)]
        arrived(acc_r, 7)
        for n in range(CHIPS):
            factor = factors[:, n : n + 1]
            for j in range(4):
                got = acc_r[n, REQ * j : REQ * j + REQ].astype(F32)
                latent[j] = latent[j] + factor * got
        latent = jnp.concatenate(latent, axis=1) / row_total

        high = latent.astype(BF16)
        rest = latent - high.astype(F32)
        middle = rest.astype(BF16)
        low = (rest - middle.astype(F32)).astype(BF16)
        parts = jnp.concatenate([high, middle, low], axis=0)
        value = mm(parts, value_up)
        low_value = mm(parts, value_down)
        value = value[:16] + value[16:32] + value[32:48]
        low_value = low_value[:16] + low_value[16:32] + low_value[32:48]
        low_value = (low_value * own_mask).astype(BF16)
        att[block_own] = (value + mm(low_value, avu_v[...])).astype(BF16)


    @pl.when(owner)
    def _():
        def send_att(i, carry):
            send(
                att.at[block_own], att.at[block_own], 8, 2 * chip_at(i) + core, group
            ).start()
            return carry

        lax.fori_loop(0, CHIPS - 1, send_att, 0)

    wait("wo", "wo share")
    all_here = pltpu.make_async_copy(att, att, recv_sem.at[8]).wait
    but_own = att.at[pl.ds(0, 15)]
    pl.when(owner)(pltpu.make_async_copy(but_own, but_own, recv_sem.at[8]).wait)
    pl.when(jnp.logical_not(owner))(all_here)
    many = acc_r.at[0, pl.ds(0, 16)]

    def all_sent():
        def one(i, carry):
            pltpu.make_async_copy(many, many, send_sem.at[8]).wait()
            return carry

        lax.fori_loop(0, CHIPS - 1, one, 0)

    pending["att out"] = lambda: pl.when(owner)(all_sent)
    rows = jnp.concatenate(
        [
            jnp.concatenate([att[2 * h], att[2 * h + 1]], axis=0)
            for h in range(HALF)
        ],
        axis=1,
    )
    for n in range(2):
        mixed = mm_t(rows, wo_v[n])
        mixed = jnp.concatenate([mixed, jnp.zeros((ROWS, 128 - WIDTH), F32)], axis=1)
        for y in range(GROUPS):
            part[n, y] = jnp.concatenate(
                [mixed[2 * y : 2 * y + 2], mixed[REQ + 2 * y : REQ + 2 * y + 2]], axis=0
            )

    def send_part(i, carry):
        y = (group + far_first(i, GROUPS)) & (GROUPS - 1)
        for n in range(2):
            send_or_keep(
                part.at[n, y], part_r.at[2 * group + core], 9, me ^ n, y
            )
        return carry

    lax.fori_loop(0, GROUPS, send_part, 0)
    arrives("part", part_r, 9)
    leaves("part out", part_r.at[pl.ds(0, 2 * GROUPS - 1)], 9)
    wait("part")
    done = part_r[0]
    for n in range(1, 2 * GROUPS):
        done = done + part_r[n]
    done = done[:, :WIDTH].astype(BF16)
    for step in range(2):
        for r in range(2):
            out_ref[r, step : step + 1, :] = done[2 * step + r : 2 * step + r + 1]

    finish()


def body(
    normed_query_latent,
    fresh_token_latent,
    prefix_latent_cache,
    query_up_weight,
    key_up_weight,
    value_up_weight,
    output_weight,
    adapter_query_down,
    adapter_query_up,
    adapter_key_down,
    adapter_key_up,
    adapter_value_down,
    adapter_value_up,
    request_adapter,
    group_first_request,
    group_request_count,
):
    operands = (
        normed_query_latent.reshape(ROWS, -1),
        fresh_token_latent.reshape(ROWS, -1),
        prefix_latent_cache.T,
        query_up_weight.T,
        jnp.transpose(key_up_weight, (0, 2, 1)),
        value_up_weight,
        output_weight.T,
        jnp.transpose(adapter_query_down, (0, 2, 1)).reshape(128, -1),
        adapter_query_up.reshape(128, COLS),
        adapter_key_down,
        adapter_key_up.reshape(128, -1),
        adapter_value_down,
        adapter_value_up.reshape(128, -1),
    )
    vmem = pltpu.VMEM
    return pl.pallas_call(
        kernel,
        out_shape=jax.ShapeDtypeStruct((2, 2, WIDTH), BF16),
        in_specs=[pl.BlockSpec(memory_space=pl.ANY)] * 13
        + [pl.BlockSpec(memory_space=pltpu.SMEM)] * 3,
        out_specs=pl.BlockSpec(memory_space=pltpu.VMEM),
        scratch_shapes=[
            vmem((ROWS, 1536), BF16),
            vmem((ROWS, LAT + ROPE), BF16),
            vmem((2, LAT + ROPE, KEYS), BF16),
            vmem((COLS, 1536), BF16),
            vmem((HEADS, 8, 128), BF16),
            vmem((HEADS, 8, 128), BF16),
            vmem((2, WIDTH, HALF * 128), BF16),
            vmem((128, 1536), BF16),
            vmem((128, COLS), BF16),
            vmem((8, 8, 16), BF16),
            vmem((128, 128), BF16),
            vmem((8, 8, 16), BF16),
            vmem((128, 128), BF16),
            vmem((HEADS, 16, 128), BF16),
            vmem((HEADS, 16, 128), BF16),
            vmem((16, 16, 128), BF16),
            vmem((CTX, 16, 128), BF16),
            vmem((ROWS, 128), BF16),
            vmem((4, ROWS, 128), BF16),
            vmem((ROWS, 128), BF16),
            vmem((16, 128), BF16),
            vmem((CHIPS, ROWS, 128), BF16),
            vmem((HALF, 16, 128), BF16),
            vmem((16, 4 * REQ, 128), BF16),
            vmem((CHIPS, 4 * REQ, 128), BF16),
            vmem((HALF, 2, 128), F32),
            vmem((CHIPS, 2, 128), F32),
            vmem((128, 128), F32),
            vmem((16, 16, 128), BF16),
            vmem((2, GROUPS, 4, 128), F32),
            vmem((2 * GROUPS, 4, 128), F32),
            pltpu.SemaphoreType.REGULAR,
            pltpu.SemaphoreType.DMA((13,)),
            pltpu.SemaphoreType.DMA((11,)),
            pltpu.SemaphoreType.DMA((13,)),
        ],
        compiler_params=pltpu.CompilerParams(
            collective_id=0, has_side_effects=True, vmem_limit_bytes=60 * 2**20
        ),
        name="latent_attention",
    )(*operands, request_adapter, group_first_request, group_request_count)


def solution(mesh):
    placed = (
        P(),
        P(),
        P("ctx", None),
        P(None, ("head", "ctx")),
        P("head", None, "ctx"),
        P("head", "ctx", None),
        P("head", "ctx"),
        P(),
        P(None, None, ("head", "ctx")),
        P(None, "ctx", None),
        P(None, None, "head"),
        P(None, "ctx", None),
        P(None, None, "head"),
        P(),
        P(),
        P(),
    )
    return jax.shard_map(
        body, mesh=mesh, in_specs=placed, out_specs=P("head", None, "ctx"), check_vma=False
    )
```

```python
import functools
import math

import jax
import jax.numpy as jnp
from jax import lax
from jax.experimental import pallas as pl
from jax.experimental.pallas import tpu as pltpu
from jax.sharding import PartitionSpec as P

MESH = pl.DeviceIdType.MESH
F32 = jnp.float32
BF16 = jnp.bfloat16

CTX = 64
CHIPS = CTX // 2
GROUPS = 8
HEADS = 16
HALF = HEADS // 2
ROWS = 32
REQ = 16
NOPE = 128
ROPE = 64
LAT = 512
COLS = 48
KEYS = 512
WIDTH = 112
PAIRS = 4
SCALE = 1.0 / math.sqrt(NOPE + ROPE)


def mm(a, b):
    return lax.dot_general(a, b, (((1,), (0,)), ((), ())), preferred_element_type=F32)


def mm_t(a, b):
    return lax.dot_general(a, b, (((1,), (1,)), ((), ())), preferred_element_type=F32)


def far_first(i, size):
    return size // 2 + ((i + 1) >> 1) * (1 - 2 * (i & 1))


def kernel(
    x_hbm,
    fresh_hbm,
    cache_hbm,
    wq_hbm,
    kup_hbm,
    vup_hbm,
    wo_hbm,
    aqd_hbm,
    aqu_hbm,
    akd_hbm,
    aku_hbm,
    avd_hbm,
    avu_hbm,
    adapter_s,
    first_s,
    count_s,
    out_ref,
    x_v,
    fresh_v,
    cache_v,
    wq_v,
    kup_v,
    vup_v,
    wo_v,
    aqd_v,
    aqu_v,
    akd_v,
    aku_v,
    avd_v,
    avu_v,
    kmsg,
    vmsg,
    kw,
    vw,
    col_s,
    qcol,
    lq_s,
    pe_s,
    lat,
    pos,
    acc_s,
    acc_r,
    ml_s,
    ml_r,
    turned,
    att,
    part,
    part_r,
    ready,
    load_sem,
    send_sem,
    recv_sem,
):
    me = lax.axis_index("ctx")
    group = lax.axis_index("head")
    chip = me >> 1
    core = me & 1
    x_at = me >> 4
    z_at = chip & 7
    place = me & 15
    head_made = me >> 2
    piece = me & 3
    head_up = 4 * (place & 3) + (place >> 2)
    up_core = head_up >> 3
    head_own = (chip ^ 4) >> 1
    block_own = (chip & 15) ^ 4
    step_own = chip & 1
    owner = core == chip >> 4

    def chip_at(i):
        dz = far_first(i >> 2, 8)
        dx = far_first(i & 3, 4)
        return (((x_at + dx) & 3) << 3) | ((z_at + dz) & 7)

    def group_of(z_there, pair):
        step = (pair - (z_there >> 1)) & 3
        nearer = 3 - 2 * (z_there & 1)
        beside = jnp.where(step == nearer, 1, 2)
        return jnp.where(step == 0, 0, jnp.where(step == 2, 3, beside))

    barrier = pltpu.get_barrier_semaphore()

    def greet(ctx, y):
        pl.semaphore_signal(barrier, inc=1, device_id=(ctx, y), device_id_type=MESH)

    def greet_plane(i, carry):
        z = (z_at + far_first(i, 8)) & 7
        greet(16 * x_at + 2 * z + core, group)
        greet(16 * x_at + 2 * z + 1 - core, group)
        return carry

    lax.fori_loop(0, 7, greet_plane, 0)
    line = [16 * ((x_at + d) & 3) + place for d in (2, 1, 3)]
    for ctx in line:
        greet(ctx, group)

    @pl.when(head_up >> 2 != x_at)
    def _():
        for n in range(4):
            greet(4 * head_up + n, group)

    def greet_group(i, carry):
        y = (group + far_first(i, GROUPS)) & (GROUPS - 1)
        greet(me, y)
        greet(me ^ 1, y)
        return carry

    lax.fori_loop(0, GROUPS - 1, greet_group, 0)
    greet(me ^ 1, group)

    up_col = pl.multiple_of(head_up * NOPE, NOPE)
    own_col = pl.multiple_of(head_own * NOPE, NOPE)
    half_col = pl.multiple_of(core * (HALF * NOPE), HALF * NOPE)
    other_col = pl.multiple_of((1 - core) * (HALF * NOPE), HALF * NOPE)
    pending = {}
    for n, (name, src, dst) in enumerate(
        (
            ("x", x_hbm, x_v),
            ("aqd", aqd_hbm, aqd_v),
            ("wq", wq_hbm, wq_v),
            ("aqu", aqu_hbm, aqu_v),
            ("kup", kup_hbm, kup_v),
            ("akd", akd_hbm, akd_v),
            ("vup", vup_hbm, vup_v),
            ("avd", avd_hbm, avd_v),
            ("aku", aku_hbm.at[:, pl.ds(up_col, NOPE)], aku_v),
            ("cache", cache_hbm, cache_v.at[0]),
            ("fresh", fresh_hbm, fresh_v),
            ("avu", avu_hbm.at[:, pl.ds(own_col, NOPE)], avu_v),
            ("wo", wo_hbm.at[:, pl.ds(half_col, HALF * NOPE)], wo_v.at[0]),
        )
    ):
        load = pltpu.make_async_copy(src, dst, load_sem.at[n])
        load.start()
        pending[name] = load.wait

    def wait(*names):
        for name in names:
            pending.pop(name)()

    def finish():
        wait(*list(pending))

    def send(src, dst, n, ctx, y, out=None):
        return pltpu.make_async_remote_copy(
            src_ref=src,
            dst_ref=dst,
            send_sem=send_sem.at[n if out is None else out],
            recv_sem=recv_sem.at[n],
            device_id=(ctx, y),
            device_id_type=MESH,
        )

    def send_or_keep(src, dst, n, ctx, y=None, out=None):
        y = group if y is None else y
        here = jnp.logical_and(ctx == me, y == group)

        @pl.when(here)
        def _():
            pltpu.make_async_copy(src, dst, recv_sem.at[n]).start()

        @pl.when(jnp.logical_not(here))
        def _():
            send(src, dst, n, ctx, y, out).start()

    def arrives(name, ref, n, when=None):
        wait_all = pltpu.make_async_copy(ref, ref, recv_sem.at[n]).wait
        pending[name] = wait_all if when is None else lambda: pl.when(when)(wait_all)

    def leaves(name, ref, n, kept=None, fewer=None):
        wait_all = pltpu.make_async_copy(ref, ref, send_sem.at[n]).wait

        def either():
            pl.when(kept)(pltpu.make_async_copy(fewer, fewer, send_sem.at[n]).wait)
            pl.when(jnp.logical_not(kept))(wait_all)

        pending[name] = wait_all if kept is None else either

    lane_adapter = lax.broadcasted_iota(jnp.int32, (REQ, 128), 1) // 16
    request = lax.broadcasted_iota(jnp.int32, (REQ, 128), 0)
    adapter = jnp.zeros((REQ, 128), jnp.int32)
    first = jnp.zeros((REQ, 128), jnp.int32)
    count = jnp.zeros((REQ, 128), jnp.int32)
    for r in range(REQ):
        adapter = jnp.where(request == r, adapter_s[r], adapter)
    for a in range(8):
        first = jnp.where(lane_adapter == a, first_s[a], first)
        count = jnp.where(lane_adapter == a, count_s[a], count)
    owns = adapter == lane_adapter
    within = request - first
    live = jnp.logical_and(owns, jnp.logical_and(within >= 0, within < count))
    own_mask = jnp.where(owns, 1.0, 0.0).astype(F32)
    live_mask = jnp.where(live, 1.0, 0.0).astype(F32)
    live_mask = jnp.concatenate([live_mask, live_mask], axis=0)

    wait("x", "aqd")
    x = x_v[...]
    low = (mm_t(x, aqd_v[...]) * live_mask).astype(BF16)
    wait("wq", "aqu")
    cols = (mm_t(x, wq_v[...]) + mm(low, aqu_v[...])).astype(BF16)
    col_s[...] = jnp.concatenate(
        [cols.astype(F32), jnp.zeros((ROWS, 128 - COLS), F32)], axis=1
    ).astype(BF16)

    wait("kup", "akd")
    table = jnp.concatenate([akd_v[a].astype(F32) for a in range(8)], axis=1)
    for h in range(HEADS):
        kmsg[h] = jnp.concatenate([kup_v[h].astype(F32), table], axis=0).astype(BF16)

    pl.semaphore_wait(barrier, 15 + 3 + 3 + 2 * (GROUPS - 1))
    for ctx in line:
        pl.semaphore_signal(ready, inc=1, device_id=(ctx, group), device_id_type=MESH)
    pending["ready"] = lambda: pl.semaphore_wait(ready, 3)

    def send_keys(i, carry):
        z = (z_at + far_first(i, 8)) & 7
        for c in range(2):
            to = 2 * z + c
            src = kmsg.at[4 * (to & 3) + (to >> 2)]
            send(src, kw.at[place], 0, 16 * x_at + to, group).start()
        return carry

    lax.fori_loop(0, 7, send_keys, 0)
    to = place ^ 1
    src = kmsg.at[4 * (to & 3) + (to >> 2)]
    send(src, kw.at[place], 0, me ^ 1, group).start()
    pltpu.make_async_copy(kmsg.at[head_up], kw.at[place], recv_sem.at[0]).start()
    arrives("kw", kw, 0)
    leaves("kw out", kw.at[pl.ds(0, 15)], 0)

    to = ((head_made & 3) << 2) | (head_made >> 2)
    for i in range(4):
        send_or_keep(
            col_s, qcol.at[piece], 2, 16 * ((x_at + (2, 1, 3, 0)[i]) & 3) + to
        )
    arrives("qcol", qcol, 2)
    leaves("qcol out", qcol, 2, piece == x_at, qcol.at[pl.ds(0, 3)])

    wait("qcol")
    q0 = qcol[0].astype(F32)
    q1 = qcol[1].astype(F32)
    q2 = qcol[2].astype(F32)
    q3 = qcol[3].astype(F32)
    nope = jnp.concatenate([q0[:, :48], q1[:, :48], q2[:, :32]], axis=1).astype(BF16)
    pe = jnp.concatenate([q2[:, 32:48], q3[:, :48]], axis=1)
    pe_s[...] = jnp.concatenate([pe[:16], pe[16:]], axis=1).astype(BF16)

    wait("ready")

    def send_pe(i, carry):
        z = (z_at + far_first(i, 8)) & 7
        n = 12 + 2 * group_of(z, z_at >> 1)
        send_or_keep(
            pe_s, pos.at[head_up & 7], n, 16 * x_at + 2 * z + up_core, out=4
        )
        return carry

    lax.fori_loop(0, 8, send_pe, 0)
    for n in range(PAIRS):
        arrives("pos %d" % n, pos.at[pl.ds(0, HALF // PAIRS)], 12 + 2 * n)
    leaves("pos out", pos, 4, core == up_core, pos.at[pl.ds(0, 7)])

    wait("aku")
    low_key = (mm_t(nope, aku_v[...]) * live_mask).astype(BF16)
    wait("kw")
    kwf = kw[...].astype(F32)
    key_up = kwf[:, :8].reshape(128, 128).astype(BF16)
    key_down = kwf[:, 8:].reshape(128, 128).astype(BF16)
    lq_s[...] = (mm_t(nope, key_up) + mm_t(low_key, key_down)).astype(BF16)

    slot = (head_up & 7) * 4 + x_at

    def send_lat(i, carry):
        there = chip_at(i)
        n = 11 + 2 * group_of(there & 7, z_at >> 1)
        send(lq_s, lat.at[slot], n, 2 * there + up_core, group, out=5).start()
        return carry

    lax.fori_loop(0, CHIPS - 1, send_lat, 0)
    send_or_keep(lq_s, lat.at[slot], 11, 2 * chip + up_core, out=5)
    leaves("lat out", lat, 5, core == up_core, lat.at[pl.ds(0, CHIPS - 1)])
    for n in range(PAIRS):
        arrives("lat %d" % n, lat.at[pl.ds(0, CHIPS // PAIRS)], 11 + 2 * n)

    share = send(cache_hbm, cache_v.at[1], 1, me ^ 1, group)
    share.start()
    pending["share"] = share.wait_recv
    pending["share out"] = share.wait_send
    share = send(
        wo_hbm.at[:, pl.ds(other_col, HALF * NOPE)], wo_v.at[1], 10, me ^ 1, group
    )
    share.start()
    pending["wo share"] = share.wait_recv
    pending["wo share out"] = share.wait_send

    wait("vup", "avd")
    table = jnp.concatenate([avd_v[a].astype(F32) for a in range(8)], axis=1)
    for h in range(HEADS):
        vmsg[h] = jnp.concatenate([vup_v[h].astype(F32), table], axis=0).astype(BF16)

    def send_values(i, carry):
        there = chip_at(i)
        send(
            vmsg.at[(there ^ 4) >> 1], vw.at[me], 3, 2 * there + (there >> 4), group
        ).start()
        return carry

    lax.fori_loop(0, CHIPS - 1, send_values, 0)
    send_or_keep(vmsg.at[head_own], vw.at[me], 3, 2 * chip + (chip >> 4))
    arrives("vw", vw, 3, owner)
    leaves(
        "vw out", vw.at[pl.ds(0, CHIPS)], 3, owner, vw.at[pl.ds(0, CHIPS - 1)]
    )

    next_pair = 2 * (z_at & 1) - 1
    pairs = [((z_at >> 1) + d) & 3 for d in (0, next_pair, -next_pair, 2)]

    def owner_of(block):
        return 2 * (16 * core + (block ^ 4)) + core

    for n_pair in range(PAIRS):
        heads = [pairs[n_pair], pairs[n_pair] + 4]
        wait("pos %d" % n_pair, "lat %d" % n_pair)
        q_lat = jnp.concatenate(
            [
                jnp.concatenate([lat[4 * h + j] for j in range(4)], axis=1)
                for h in heads
            ],
            axis=0,
        )
        q_pe = []
        for h in heads:
            both = pos[h].astype(F32)
            q_pe += [both[:, :ROPE], both[:, ROPE:]]
        q_pe = jnp.concatenate(q_pe, axis=0).astype(BF16)
        if n_pair == 0:
            wait("cache", "share")
        scores = [
            (mm(q_lat, cache_v[n, :LAT]) + mm(q_pe, cache_v[n, LAT:])) * SCALE
            for n in range(2)
        ]
        top = jnp.maximum(
            jnp.max(scores[0], axis=1, keepdims=True),
            jnp.max(scores[1], axis=1, keepdims=True),
        )
        weights = [jnp.exp(s - top) for s in scores]
        total = jnp.sum(weights[0], axis=1, keepdims=True) + jnp.sum(
            weights[1], axis=1, keepdims=True
        )
        lane = lax.broadcasted_iota(jnp.int32, (2 * ROWS, 128), 1)
        stats = jnp.where(lane == 0, top, jnp.where(lane == 1, total, 0.0))
        stats = jnp.concatenate([stats, stats], axis=0).T[:2]
        for n, h in enumerate(heads):
            ml_s[h] = stats if n == 0 else pltpu.roll(stats, 128 - 32 * n, 1)

        for h in heads:
            for step in range(2):
                send_or_keep(ml_s.at[h], ml_r.at[chip], 6, owner_of(2 * h + step))

        summed = sum(mm_t(weights[n].astype(BF16), cache_v[n, :LAT]) for n in range(2))
        for n, h in enumerate(heads):
            for step in range(2):
                rows = summed[32 * n + 16 * step : 32 * n + 16 * step + 16]
                for j in range(4):
                    acc_s[2 * h + step, 16 * j : 16 * j + 16] = rows[
                        :, 128 * j : 128 * j + 128
                    ].astype(BF16)

        for h in heads:
            for step in range(2):
                block = 2 * h + step
                send_or_keep(acc_s.at[block], acc_r.at[chip], 7, owner_of(block))

    arrives("ml", ml_r, 6, owner)
    leaves("ml out", ml_r.at[pl.ds(0, 16)], 6, owner, ml_r.at[pl.ds(0, 15)])
    arrives("acc", acc_r, 7, owner)
    leaves("acc out", acc_r.at[pl.ds(0, 16)], 7, owner, acc_r.at[pl.ds(0, 15)])

    wait("fresh", "avu")
    for name in ("vw", "ml", "acc"):
        pending.pop(name)

    def arrived(ref, n):
        pltpu.make_async_copy(ref, ref, recv_sem.at[n]).wait()

    @pl.when(owner)
    def _():
        fresh = fresh_v[...]
        own = head_own & 7
        own_rows = pl.ds(pl.multiple_of(REQ * step_own, REQ), REQ)
        own_lat = jnp.concatenate([lat[4 * own + j, own_rows] for j in range(4)], axis=1)
        both = pos[own].astype(F32)
        own_pe = jnp.where(step_own == 0, both[:, :ROPE], both[:, ROPE:]).astype(BF16)
        own_scores = (
            mm_t(own_lat, fresh[:, :LAT]) + mm_t(own_pe, fresh[:, LAT:])
        ) * SCALE
        row = lax.broadcasted_iota(jnp.int32, (REQ, ROWS), 0)
        key = lax.broadcasted_iota(jnp.int32, (REQ, ROWS), 1)
        seen = jnp.logical_and(row == key % REQ, key // REQ <= step_own)
        own_scores = jnp.where(seen, own_scores, -jnp.inf)
        own_top = jnp.max(own_scores, axis=1, keepdims=True)
        own_weights = jnp.exp(own_scores - own_top)
        own_total = jnp.sum(own_weights, axis=1, keepdims=True)
        own_sum = mm(own_weights.astype(BF16), fresh[:, :LAT])

        arrived(vw, 3)
        vwf = vw[...].astype(F32)
        value_up = vwf[:, :8].reshape(LAT, 128).astype(BF16)
        value_down = vwf[:, 8:].reshape(LAT, 128).astype(BF16)

        arrived(ml_r, 6)
        ml = ml_r[...]
        turned[...] = jnp.concatenate(
            [ml[:, 0], ml[:, 1], jnp.zeros((64, 128), F32)], axis=0
        ).T
        stats = turned[pl.ds(pl.multiple_of(REQ * step_own, REQ), REQ), :]
        tops = stats[:, :CHIPS]
        totals = stats[:, CHIPS : 2 * CHIPS]
        joined = jnp.maximum(jnp.max(tops, axis=1, keepdims=True), own_top)
        factors = jnp.exp(tops - joined)
        own_factor = jnp.exp(own_top - joined)
        row_total = (
            jnp.sum(factors * totals, axis=1, keepdims=True) + own_factor * own_total
        )
        latent = own_sum * own_factor
        latent = [latent[:, 128 * j : 128 * j + 128] for j in range(4)]
        arrived(acc_r, 7)
        for n in range(CHIPS):
            factor = factors[:, n : n + 1]
            for j in range(4):
                got = acc_r[n, REQ * j : REQ * j + REQ].astype(F32)
                latent[j] = latent[j] + factor * got
        latent = jnp.concatenate(latent, axis=1) / row_total

        high = latent.astype(BF16)
        rest = latent - high.astype(F32)
        middle = rest.astype(BF16)
        low = (rest - middle.astype(F32)).astype(BF16)
        parts = jnp.concatenate([high, middle, low], axis=0)
        value = mm(parts, value_up)
        low_value = mm(parts, value_down)
        value = value[:16] + value[16:32] + value[32:48]
        low_value = low_value[:16] + low_value[16:32] + low_value[32:48]
        low_value = (low_value * own_mask).astype(BF16)
        att[block_own] = (value + mm(low_value, avu_v[...])).astype(BF16)


    @pl.when(owner)
    def _():
        def send_att(i, carry):
            send(
                att.at[block_own], att.at[block_own], 8, 2 * chip_at(i) + core, group
            ).start()
            return carry

        lax.fori_loop(0, CHIPS - 1, send_att, 0)

    wait("wo", "wo share")
    all_here = pltpu.make_async_copy(att, att, recv_sem.at[8]).wait
    but_own = att.at[pl.ds(0, 15)]
    pl.when(owner)(pltpu.make_async_copy(but_own, but_own, recv_sem.at[8]).wait)
    pl.when(jnp.logical_not(owner))(all_here)
    many = acc_r.at[0, pl.ds(0, 16)]

    def all_sent():
        def one(i, carry):
            pltpu.make_async_copy(many, many, send_sem.at[8]).wait()
            return carry

        lax.fori_loop(0, CHIPS - 1, one, 0)

    pending["att out"] = lambda: pl.when(owner)(all_sent)
    rows = jnp.concatenate(
        [
            jnp.concatenate([att[2 * h], att[2 * h + 1]], axis=0)
            for h in range(HALF)
        ],
        axis=1,
    )
    for n in range(2):
        mixed = mm_t(rows, wo_v[n])
        mixed = jnp.concatenate([mixed, jnp.zeros((ROWS, 128 - WIDTH), F32)], axis=1)
        for y in range(GROUPS):
            part[n, y] = jnp.concatenate(
                [mixed[2 * y : 2 * y + 2], mixed[REQ + 2 * y : REQ + 2 * y + 2]], axis=0
            )

    def send_part(i, carry):
        y = (group + far_first(i, GROUPS)) & (GROUPS - 1)
        for n in range(2):
            send(part.at[n, y], part_r.at[2 * group + core], 9, me ^ n, y).start()
        return carry

    lax.fori_loop(0, GROUPS - 1, send_part, 0)
    send(part.at[1, group], part_r.at[2 * group + core], 9, me ^ 1, group).start()
    pltpu.make_async_copy(
        part.at[0, group], part_r.at[2 * group + core], recv_sem.at[9]
    ).start()
    arrives("part", part_r, 9)
    leaves("part out", part_r.at[pl.ds(0, 2 * GROUPS - 1)], 9)
    wait("part")
    done = part_r[0]
    for n in range(1, 2 * GROUPS):
        done = done + part_r[n]
    done = done[:, :WIDTH].astype(BF16)
    for step in range(2):
        for r in range(2):
            out_ref[r, step : step + 1, :] = done[2 * step + r : 2 * step + r + 1]

    finish()


def body(
    normed_query_latent,
    fresh_token_latent,
    prefix_latent_cache,
    query_up_weight,
    key_up_weight,
    value_up_weight,
    output_weight,
    adapter_query_down,
    adapter_query_up,
    adapter_key_down,
    adapter_key_up,
    adapter_value_down,
    adapter_value_up,
    request_adapter,
    group_first_request,
    group_request_count,
):
    operands = (
        normed_query_latent.reshape(ROWS, -1),
        fresh_token_latent.reshape(ROWS, -1),
        prefix_latent_cache.T,
        query_up_weight.T,
        jnp.transpose(key_up_weight, (0, 2, 1)),
        value_up_weight,
        output_weight.T,
        jnp.transpose(adapter_query_down, (0, 2, 1)).reshape(128, -1),
        adapter_query_up.reshape(128, COLS),
        adapter_key_down,
        adapter_key_up.reshape(128, -1),
        adapter_value_down,
        adapter_value_up.reshape(128, -1),
    )
    vmem = pltpu.VMEM
    return pl.pallas_call(
        kernel,
        out_shape=jax.ShapeDtypeStruct((2, 2, WIDTH), BF16),
        in_specs=[pl.BlockSpec(memory_space=pl.ANY)] * 13
        + [pl.BlockSpec(memory_space=pltpu.SMEM)] * 3,
        out_specs=pl.BlockSpec(memory_space=pltpu.VMEM),
        scratch_shapes=[
            vmem((ROWS, 1536), BF16),
            vmem((ROWS, LAT + ROPE), BF16),
            vmem((2, LAT + ROPE, KEYS), BF16),
            vmem((COLS, 1536), BF16),
            vmem((HEADS, 8, 128), BF16),
            vmem((HEADS, 8, 128), BF16),
            vmem((2, WIDTH, HALF * 128), BF16),
            vmem((128, 1536), BF16),
            vmem((128, COLS), BF16),
            vmem((8, 8, 16), BF16),
            vmem((128, 128), BF16),
            vmem((8, 8, 16), BF16),
            vmem((128, 128), BF16),
            vmem((HEADS, 16, 128), BF16),
            vmem((HEADS, 16, 128), BF16),
            vmem((16, 16, 128), BF16),
            vmem((CTX, 16, 128), BF16),
            vmem((ROWS, 128), BF16),
            vmem((4, ROWS, 128), BF16),
            vmem((ROWS, 128), BF16),
            vmem((16, 128), BF16),
            vmem((CHIPS, ROWS, 128), BF16),
            vmem((HALF, 16, 128), BF16),
            vmem((16, 4 * REQ, 128), BF16),
            vmem((CHIPS, 4 * REQ, 128), BF16),
            vmem((HALF, 2, 128), F32),
            vmem((CHIPS, 2, 128), F32),
            vmem((128, 128), F32),
            vmem((16, 16, 128), BF16),
            vmem((2, GROUPS, 4, 128), F32),
            vmem((2 * GROUPS, 4, 128), F32),
            pltpu.SemaphoreType.REGULAR,
            pltpu.SemaphoreType.DMA((13,)),
            pltpu.SemaphoreType.DMA((11,)),
            pltpu.SemaphoreType.DMA((19,)),
        ],
        compiler_params=pltpu.CompilerParams(
            collective_id=0, has_side_effects=True, vmem_limit_bytes=60 * 2**20
        ),
        name="latent_attention",
    )(*operands, request_adapter, group_first_request, group_request_count)


def solution(mesh):
    placed = (
        P(),
        P(),
        P("ctx", None),
        P(None, ("head", "ctx")),
        P("head", None, "ctx"),
        P("head", "ctx", None),
        P("head", "ctx"),
        P(),
        P(None, None, ("head", "ctx")),
        P(None, "ctx", None),
        P(None, None, "head"),
        P(None, "ctx", None),
        P(None, None, "head"),
        P(),
        P(),
        P(),
    )
    return jax.shard_map(
        body, mesh=mesh, in_specs=placed, out_specs=P("head", None, "ctx"), check_vma=False
    )
```

```python
import functools
import math

import jax
import jax.numpy as jnp
from jax import lax
from jax.experimental import pallas as pl
from jax.experimental.pallas import tpu as pltpu
from jax.sharding import PartitionSpec as P

MESH = pl.DeviceIdType.MESH
F32 = jnp.float32
BF16 = jnp.bfloat16

CTX = 64
CHIPS = CTX // 2
GROUPS = 8
HEADS = 16
HALF = HEADS // 2
ROWS = 32
REQ = 16
NOPE = 128
ROPE = 64
LAT = 512
COLS = 48
KEYS = 512
WIDTH = 112
PAIRS = 4
SCALE = 1.0 / math.sqrt(NOPE + ROPE)


def mm(a, b):
    return lax.dot_general(a, b, (((1,), (0,)), ((), ())), preferred_element_type=F32)


def mm_t(a, b):
    return lax.dot_general(a, b, (((1,), (1,)), ((), ())), preferred_element_type=F32)


def far_first(i, size):
    return size // 2 + ((i + 1) >> 1) * (1 - 2 * (i & 1))


def kernel(
    x_hbm,
    fresh_hbm,
    cache_hbm,
    wq_hbm,
    kup_hbm,
    vup_hbm,
    wo_hbm,
    aqd_hbm,
    aqu_hbm,
    akd_hbm,
    aku_hbm,
    avd_hbm,
    avu_hbm,
    adapter_s,
    first_s,
    count_s,
    out_ref,
    x_v,
    fresh_v,
    cache_v,
    wq_v,
    kup_v,
    vup_v,
    wo_v,
    aqd_v,
    aqu_v,
    akd_v,
    aku_v,
    avd_v,
    avu_v,
    kmsg,
    vmsg,
    kw,
    vw,
    col_s,
    qcol,
    lq_s,
    pe_s,
    lat,
    pos,
    acc_s,
    acc_r,
    ml_s,
    ml_r,
    turned,
    att,
    part,
    part_r,
    ready,
    load_sem,
    send_sem,
    recv_sem,
):
    me = lax.axis_index("ctx")
    group = lax.axis_index("head")
    chip = me >> 1
    core = me & 1
    x_at = me >> 4
    z_at = chip & 7
    place = me & 15
    head_made = me >> 2
    piece = me & 3
    head_up = 4 * (place & 3) + (place >> 2)
    up_core = head_up >> 3
    head_own = (chip ^ 4) >> 1
    block_own = (chip & 15) ^ 4
    step_own = chip & 1
    owner = core == chip >> 4

    def chip_at(i):
        dz = far_first(i >> 2, 8)
        dx = far_first(i & 3, 4)
        return (((x_at + dx) & 3) << 3) | ((z_at + dz) & 7)

    def group_of(z_there, pair):
        step = (pair - (z_there >> 1)) & 3
        nearer = 3 - 2 * (z_there & 1)
        beside = jnp.where(step == nearer, 1, 2)
        return jnp.where(step == 0, 0, jnp.where(step == 2, 3, beside))

    barrier = pltpu.get_barrier_semaphore()

    def greet(ctx, y):
        pl.semaphore_signal(barrier, inc=1, device_id=(ctx, y), device_id_type=MESH)

    def greet_plane(i, carry):
        z = (z_at + far_first(i, 8)) & 7
        greet(16 * x_at + 2 * z + core, group)
        greet(16 * x_at + 2 * z + 1 - core, group)
        return carry

    lax.fori_loop(0, 7, greet_plane, 0)
    line = [16 * ((x_at + d) & 3) + place for d in (2, 1, 3)]
    for ctx in line:
        greet(ctx, group)

    @pl.when(head_up >> 2 != x_at)
    def _():
        for n in range(4):
            greet(4 * head_up + n, group)

    def greet_group(i, carry):
        y = (group + far_first(i, GROUPS)) & (GROUPS - 1)
        greet(me, y)
        greet(me ^ 1, y)
        return carry

    lax.fori_loop(0, GROUPS - 1, greet_group, 0)
    greet(me ^ 1, group)

    up_col = pl.multiple_of(head_up * NOPE, NOPE)
    own_col = pl.multiple_of(head_own * NOPE, NOPE)
    half_col = pl.multiple_of(core * (HALF * NOPE), HALF * NOPE)
    other_col = pl.multiple_of((1 - core) * (HALF * NOPE), HALF * NOPE)
    pending = {}
    for n, (name, src, dst) in enumerate(
        (
            ("x", x_hbm, x_v),
            ("aqd", aqd_hbm, aqd_v),
            ("wq", wq_hbm, wq_v),
            ("aqu", aqu_hbm, aqu_v),
            ("kup", kup_hbm, kup_v),
            ("akd", akd_hbm, akd_v),
            ("vup", vup_hbm, vup_v),
            ("avd", avd_hbm, avd_v),
            ("aku", aku_hbm.at[:, pl.ds(up_col, NOPE)], aku_v),
            ("cache", cache_hbm, cache_v.at[0]),
            ("fresh", fresh_hbm, fresh_v),
            ("avu", avu_hbm.at[:, pl.ds(own_col, NOPE)], avu_v),
            ("wo", wo_hbm.at[:, pl.ds(half_col, HALF * NOPE)], wo_v.at[0]),
        )
    ):
        load = pltpu.make_async_copy(src, dst, load_sem.at[n])
        load.start()
        pending[name] = load.wait

    def wait(*names):
        for name in names:
            pending.pop(name)()

    def finish():
        wait(*list(pending))

    def send(src, dst, n, ctx, y, out=None):
        return pltpu.make_async_remote_copy(
            src_ref=src,
            dst_ref=dst,
            send_sem=send_sem.at[n if out is None else out],
            recv_sem=recv_sem.at[n],
            device_id=(ctx, y),
            device_id_type=MESH,
        )

    def send_or_keep(src, dst, n, ctx, y=None, out=None):
        y = group if y is None else y
        here = jnp.logical_and(ctx == me, y == group)

        @pl.when(here)
        def _():
            pltpu.make_async_copy(src, dst, recv_sem.at[n]).start()

        @pl.when(jnp.logical_not(here))
        def _():
            send(src, dst, n, ctx, y, out).start()

    def arrives(name, ref, n, when=None):
        wait_all = pltpu.make_async_copy(ref, ref, recv_sem.at[n]).wait
        pending[name] = wait_all if when is None else lambda: pl.when(when)(wait_all)

    def leaves(name, ref, n, kept=None, fewer=None):
        wait_all = pltpu.make_async_copy(ref, ref, send_sem.at[n]).wait

        def either():
            pl.when(kept)(pltpu.make_async_copy(fewer, fewer, send_sem.at[n]).wait)
            pl.when(jnp.logical_not(kept))(wait_all)

        pending[name] = wait_all if kept is None else either

    lane_adapter = lax.broadcasted_iota(jnp.int32, (REQ, 128), 1) // 16
    request = lax.broadcasted_iota(jnp.int32, (REQ, 128), 0)
    adapter = jnp.zeros((REQ, 128), jnp.int32)
    first = jnp.zeros((REQ, 128), jnp.int32)
    count = jnp.zeros((REQ, 128), jnp.int32)
    for r in range(REQ):
        adapter = jnp.where(request == r, adapter_s[r], adapter)
    for a in range(8):
        first = jnp.where(lane_adapter == a, first_s[a], first)
        count = jnp.where(lane_adapter == a, count_s[a], count)
    owns = adapter == lane_adapter
    within = request - first
    live = jnp.logical_and(owns, jnp.logical_and(within >= 0, within < count))
    own_mask = jnp.where(owns, 1.0, 0.0).astype(F32)
    live_mask = jnp.where(live, 1.0, 0.0).astype(F32)
    live_mask = jnp.concatenate([live_mask, live_mask], axis=0)

    wait("x", "aqd")
    x = x_v[...]
    low = (mm_t(x, aqd_v[...]) * live_mask).astype(BF16)
    wait("wq", "aqu")
    cols = (mm_t(x, wq_v[...]) + mm(low, aqu_v[...])).astype(BF16)
    col_s[...] = jnp.concatenate(
        [cols.astype(F32), jnp.zeros((ROWS, 128 - COLS), F32)], axis=1
    ).astype(BF16)

    wait("kup", "akd")
    table = jnp.concatenate([akd_v[a].astype(F32) for a in range(8)], axis=1)
    for h in range(HEADS):
        kmsg[h] = jnp.concatenate([kup_v[h].astype(F32), table], axis=0).astype(BF16)

    pl.semaphore_wait(barrier, 15 + 3 + 3 + 2 * (GROUPS - 1))
    for ctx in line:
        pl.semaphore_signal(ready, inc=1, device_id=(ctx, group), device_id_type=MESH)
    pending["ready"] = lambda: pl.semaphore_wait(ready, 3)

    def send_keys(i, carry):
        z = (z_at + far_first(i, 8)) & 7
        for c in range(2):
            to = 2 * z + c
            src = kmsg.at[4 * (to & 3) + (to >> 2)]
            send(src, kw.at[place], 0, 16 * x_at + to, group).start()
        return carry

    lax.fori_loop(0, 7, send_keys, 0)
    to = place ^ 1
    src = kmsg.at[4 * (to & 3) + (to >> 2)]
    send(src, kw.at[place], 0, me ^ 1, group).start()
    pltpu.make_async_copy(kmsg.at[head_up], kw.at[place], recv_sem.at[0]).start()
    arrives("kw", kw, 0)
    leaves("kw out", kw.at[pl.ds(0, 15)], 0)

    to = ((head_made & 3) << 2) | (head_made >> 2)
    for i in range(4):
        send_or_keep(
            col_s, qcol.at[piece], 2, 16 * ((x_at + (2, 1, 3, 0)[i]) & 3) + to
        )
    arrives("qcol", qcol, 2)
    leaves("qcol out", qcol, 2, piece == x_at, qcol.at[pl.ds(0, 3)])

    wait("qcol")
    q0 = qcol[0].astype(F32)
    q1 = qcol[1].astype(F32)
    q2 = qcol[2].astype(F32)
    q3 = qcol[3].astype(F32)
    nope = jnp.concatenate([q0[:, :48], q1[:, :48], q2[:, :32]], axis=1).astype(BF16)
    pe = jnp.concatenate([q2[:, 32:48], q3[:, :48]], axis=1)
    pe_s[...] = jnp.concatenate([pe[:16], pe[16:]], axis=1).astype(BF16)

    wait("ready")

    def send_pe(i, carry):
        z = (z_at + far_first(i, 8)) & 7
        n = 12 + 2 * group_of(z, z_at >> 1)
        send_or_keep(
            pe_s, pos.at[head_up & 7], n, 16 * x_at + 2 * z + up_core, out=4
        )
        return carry

    lax.fori_loop(0, 8, send_pe, 0)
    for n in range(PAIRS):
        arrives("pos %d" % n, pos.at[pl.ds(0, HALF // PAIRS)], 12 + 2 * n)
    leaves("pos out", pos, 4, core == up_core, pos.at[pl.ds(0, 7)])

    wait("aku")
    low_key = (mm_t(nope, aku_v[...]) * live_mask).astype(BF16)
    wait("kw")
    kwf = kw[...].astype(F32)
    key_up = kwf[:, :8].reshape(128, 128).astype(BF16)
    key_down = kwf[:, 8:].reshape(128, 128).astype(BF16)
    lq_s[...] = (mm_t(nope, key_up) + mm_t(low_key, key_down)).astype(BF16)

    slot = (head_up & 7) * 4 + x_at

    def send_lat(i, carry):
        there = chip_at(i)
        n = 11 + 2 * group_of(there & 7, z_at >> 1)
        send(lq_s, lat.at[slot], n, 2 * there + up_core, group, out=5).start()
        return carry

    def send_lat_far(i, carry):
        z = (z_at + far_first(i, 8)) & 7
        to = 16 * x_at + 2 * z + up_core
        send(lq_s, lat.at[slot], 19, to, group, out=5).start()
        return carry

    lax.fori_loop(0, 3, send_lat_far, 0)
    lax.fori_loop(12, CHIPS - 1, send_lat, 0)
    send_or_keep(lq_s, lat.at[slot], 11, 2 * chip + up_core, out=5)
    leaves("lat out", lat.at[pl.ds(0, 23)], 5, core == up_core, lat.at[pl.ds(0, 22)])
    for n in range(2):
        arrives("lat %d" % n, lat.at[pl.ds(0, 8)], 11 + 2 * n)
    arrives("lat 3", lat.at[pl.ds(0, 6)], 17)
    facing = (z_at & 1) == core
    six = lat.at[pl.ds(0, 6)]
    eight = lat.at[pl.ds(0, 8)]

    def wait_beside():
        pl.when(facing)(pltpu.make_async_copy(eight, eight, recv_sem.at[15]).wait)
        pl.when(jnp.logical_not(facing))(
            pltpu.make_async_copy(six, six, recv_sem.at[15]).wait
        )

    pending["lat 2"] = wait_beside

    share = send(cache_hbm, cache_v.at[1], 1, me ^ 1, group)
    share.start()
    pending["share"] = share.wait_recv
    pending["share out"] = share.wait_send
    share = send(
        wo_hbm.at[:, pl.ds(other_col, HALF * NOPE)], wo_v.at[1], 10, me ^ 1, group
    )
    share.start()
    pending["wo share"] = share.wait_recv
    pending["wo share out"] = share.wait_send

    wait("vup", "avd")
    table = jnp.concatenate([avd_v[a].astype(F32) for a in range(8)], axis=1)
    for h in range(HEADS):
        vmsg[h] = jnp.concatenate([vup_v[h].astype(F32), table], axis=0).astype(BF16)

    def send_values(i, carry):
        there = chip_at(i)
        send(
            vmsg.at[(there ^ 4) >> 1], vw.at[me], 3, 2 * there + (there >> 4), group
        ).start()
        return carry

    lax.fori_loop(0, CHIPS - 1, send_values, 0)
    send_or_keep(vmsg.at[head_own], vw.at[me], 3, 2 * chip + (chip >> 4))
    arrives("vw", vw, 3, owner)
    leaves(
        "vw out", vw.at[pl.ds(0, CHIPS)], 3, owner, vw.at[pl.ds(0, CHIPS - 1)]
    )

    def pass_on(*steps):
        came = lat.at[pl.ds(0, 2 * len(steps))]
        pltpu.make_async_copy(came, came, recv_sem.at[19]).wait()
        for step in steps:
            z = (z_at + step) & 7
            for c in range(2):
                made = 4 * ((2 * z + c) & 3) + (z >> 1)
                row = (made & 7) * 4 + x_at
                n = 11 + 2 * group_of(z_at, z >> 1)
                for dx in (2, 1, 3):
                    to = 16 * ((x_at + dx) & 3) + 2 * z_at + core
                    send(lat.at[row], lat.at[row], n, to, group, out=11).start()

    pl.when(facing)(lambda: pass_on(4))
    pl.when(jnp.logical_not(facing))(lambda: pass_on(3, 5))
    leaves("passed out", lat.at[pl.ds(0, 12)], 11, facing, lat.at[pl.ds(0, 6)])

    next_pair = 2 * (z_at & 1) - 1
    pairs = [((z_at >> 1) + d) & 3 for d in (0, next_pair, -next_pair, 2)]

    def owner_of(block):
        return 2 * (16 * core + (block ^ 4)) + core

    for n_pair in range(PAIRS):
        heads = [pairs[n_pair], pairs[n_pair] + 4]
        wait("pos %d" % n_pair, "lat %d" % n_pair)
        q_lat = jnp.concatenate(
            [
                jnp.concatenate([lat[4 * h + j] for j in range(4)], axis=1)
                for h in heads
            ],
            axis=0,
        )
        q_pe = []
        for h in heads:
            both = pos[h].astype(F32)
            q_pe += [both[:, :ROPE], both[:, ROPE:]]
        q_pe = jnp.concatenate(q_pe, axis=0).astype(BF16)
        if n_pair == 0:
            wait("cache", "share")
        scores = [
            (mm(q_lat, cache_v[n, :LAT]) + mm(q_pe, cache_v[n, LAT:])) * SCALE
            for n in range(2)
        ]
        top = jnp.maximum(
            jnp.max(scores[0], axis=1, keepdims=True),
            jnp.max(scores[1], axis=1, keepdims=True),
        )
        weights = [jnp.exp(s - top) for s in scores]
        total = jnp.sum(weights[0], axis=1, keepdims=True) + jnp.sum(
            weights[1], axis=1, keepdims=True
        )
        lane = lax.broadcasted_iota(jnp.int32, (2 * ROWS, 128), 1)
        stats = jnp.where(lane == 0, top, jnp.where(lane == 1, total, 0.0))
        stats = jnp.concatenate([stats, stats], axis=0).T[:2]
        for n, h in enumerate(heads):
            ml_s[h] = stats if n == 0 else pltpu.roll(stats, 128 - 32 * n, 1)

        for h in heads:
            for step in range(2):
                send_or_keep(ml_s.at[h], ml_r.at[chip], 6, owner_of(2 * h + step))

        summed = sum(mm_t(weights[n].astype(BF16), cache_v[n, :LAT]) for n in range(2))
        for n, h in enumerate(heads):
            for step in range(2):
                rows = summed[32 * n + 16 * step : 32 * n + 16 * step + 16]
                for j in range(4):
                    acc_s[2 * h + step, 16 * j : 16 * j + 16] = rows[
                        :, 128 * j : 128 * j + 128
                    ].astype(BF16)

        for h in heads:
            for step in range(2):
                block = 2 * h + step
                send_or_keep(acc_s.at[block], acc_r.at[chip], 7, owner_of(block))

    arrives("ml", ml_r, 6, owner)
    leaves("ml out", ml_r.at[pl.ds(0, 16)], 6, owner, ml_r.at[pl.ds(0, 15)])
    arrives("acc", acc_r, 7, owner)
    leaves("acc out", acc_r.at[pl.ds(0, 16)], 7, owner, acc_r.at[pl.ds(0, 15)])

    wait("fresh", "avu")
    for name in ("vw", "ml", "acc"):
        pending.pop(name)

    def arrived(ref, n):
        pltpu.make_async_copy(ref, ref, recv_sem.at[n]).wait()

    @pl.when(owner)
    def _():
        fresh = fresh_v[...]
        own = head_own & 7
        own_rows = pl.ds(pl.multiple_of(REQ * step_own, REQ), REQ)
        own_lat = jnp.concatenate([lat[4 * own + j, own_rows] for j in range(4)], axis=1)
        both = pos[own].astype(F32)
        own_pe = jnp.where(step_own == 0, both[:, :ROPE], both[:, ROPE:]).astype(BF16)
        own_scores = (
            mm_t(own_lat, fresh[:, :LAT]) + mm_t(own_pe, fresh[:, LAT:])
        ) * SCALE
        row = lax.broadcasted_iota(jnp.int32, (REQ, ROWS), 0)
        key = lax.broadcasted_iota(jnp.int32, (REQ, ROWS), 1)
        seen = jnp.logical_and(row == key % REQ, key // REQ <= step_own)
        own_scores = jnp.where(seen, own_scores, -jnp.inf)
        own_top = jnp.max(own_scores, axis=1, keepdims=True)
        own_weights = jnp.exp(own_scores - own_top)
        own_total = jnp.sum(own_weights, axis=1, keepdims=True)
        own_sum = mm(own_weights.astype(BF16), fresh[:, :LAT])

        arrived(vw, 3)
        vwf = vw[...].astype(F32)
        value_up = vwf[:, :8].reshape(LAT, 128).astype(BF16)
        value_down = vwf[:, 8:].reshape(LAT, 128).astype(BF16)

        arrived(ml_r, 6)
        ml = ml_r[...]
        turned[...] = jnp.concatenate(
            [ml[:, 0], ml[:, 1], jnp.zeros((64, 128), F32)], axis=0
        ).T
        stats = turned[pl.ds(pl.multiple_of(REQ * step_own, REQ), REQ), :]
        tops = stats[:, :CHIPS]
        totals = stats[:, CHIPS : 2 * CHIPS]
        joined = jnp.maximum(jnp.max(tops, axis=1, keepdims=True), own_top)
        factors = jnp.exp(tops - joined)
        own_factor = jnp.exp(own_top - joined)
        row_total = (
            jnp.sum(factors * totals, axis=1, keepdims=True) + own_factor * own_total
        )
        latent = own_sum * own_factor
        latent = [latent[:, 128 * j : 128 * j + 128] for j in range(4)]
        arrived(acc_r, 7)
        for n in range(CHIPS):
            factor = factors[:, n : n + 1]
            for j in range(4):
                got = acc_r[n, REQ * j : REQ * j + REQ].astype(F32)
                latent[j] = latent[j] + factor * got
        latent = jnp.concatenate(latent, axis=1) / row_total

        high = latent.astype(BF16)
        rest = latent - high.astype(F32)
        middle = rest.astype(BF16)
        low = (rest - middle.astype(F32)).astype(BF16)
        parts = jnp.concatenate([high, middle, low], axis=0)
        value = mm(parts, value_up)
        low_value = mm(parts, value_down)
        value = value[:16] + value[16:32] + value[32:48]
        low_value = low_value[:16] + low_value[16:32] + low_value[32:48]
        low_value = (low_value * own_mask).astype(BF16)
        att[block_own] = (value + mm(low_value, avu_v[...])).astype(BF16)


    @pl.when(owner)
    def _():
        def send_att(i, carry):
            send(
                att.at[block_own], att.at[block_own], 8, 2 * chip_at(i) + core, group
            ).start()
            return carry

        lax.fori_loop(0, CHIPS - 1, send_att, 0)

    wait("wo", "wo share")
    all_here = pltpu.make_async_copy(att, att, recv_sem.at[8]).wait
    but_own = att.at[pl.ds(0, 15)]
    pl.when(owner)(pltpu.make_async_copy(but_own, but_own, recv_sem.at[8]).wait)
    pl.when(jnp.logical_not(owner))(all_here)
    many = vw.at[pl.ds(0, CHIPS - 1)]
    all_sent = pltpu.make_async_copy(many, many, send_sem.at[8]).wait
    pending["att out"] = lambda: pl.when(owner)(all_sent)
    rows = jnp.concatenate(
        [
            jnp.concatenate([att[2 * h], att[2 * h + 1]], axis=0)
            for h in range(HALF)
        ],
        axis=1,
    )
    for n in range(2):
        mixed = mm_t(rows, wo_v[n])
        mixed = jnp.concatenate([mixed, jnp.zeros((ROWS, 128 - WIDTH), F32)], axis=1)
        for y in range(GROUPS):
            part[n, y] = jnp.concatenate(
                [mixed[2 * y : 2 * y + 2], mixed[REQ + 2 * y : REQ + 2 * y + 2]], axis=0
            )

    def send_part(i, carry):
        y = (group + far_first(i, GROUPS)) & (GROUPS - 1)
        for n in range(2):
            send(part.at[n, y], part_r.at[2 * group + core], 9, me ^ n, y).start()
        return carry

    lax.fori_loop(0, GROUPS - 1, send_part, 0)
    send(part.at[1, group], part_r.at[2 * group + core], 9, me ^ 1, group).start()
    pltpu.make_async_copy(
        part.at[0, group], part_r.at[2 * group + core], recv_sem.at[9]
    ).start()
    finish()
    arrives("part", part_r, 9)
    leaves("part out", part_r.at[pl.ds(0, 2 * GROUPS - 1)], 9)
    wait("part")
    done = part_r[0]
    for n in range(1, 2 * GROUPS):
        done = done + part_r[n]
    done = done[:, :WIDTH].astype(BF16)
    for step in range(2):
        for r in range(2):
            out_ref[r, step : step + 1, :] = done[2 * step + r : 2 * step + r + 1]

    finish()


def body(
    normed_query_latent,
    fresh_token_latent,
    prefix_latent_cache,
    query_up_weight,
    key_up_weight,
    value_up_weight,
    output_weight,
    adapter_query_down,
    adapter_query_up,
    adapter_key_down,
    adapter_key_up,
    adapter_value_down,
    adapter_value_up,
    request_adapter,
    group_first_request,
    group_request_count,
):
    operands = (
        normed_query_latent.reshape(ROWS, -1),
        fresh_token_latent.reshape(ROWS, -1),
        prefix_latent_cache.T,
        query_up_weight.T,
        jnp.transpose(key_up_weight, (0, 2, 1)),
        value_up_weight,
        output_weight.T,
        jnp.transpose(adapter_query_down, (0, 2, 1)).reshape(128, -1),
        adapter_query_up.reshape(128, COLS),
        adapter_key_down,
        adapter_key_up.reshape(128, -1),
        adapter_value_down,
        adapter_value_up.reshape(128, -1),
    )
    vmem = pltpu.VMEM
    return pl.pallas_call(
        kernel,
        out_shape=jax.ShapeDtypeStruct((2, 2, WIDTH), BF16),
        in_specs=[pl.BlockSpec(memory_space=pl.ANY)] * 13
        + [pl.BlockSpec(memory_space=pltpu.SMEM)] * 3,
        out_specs=pl.BlockSpec(memory_space=pltpu.VMEM),
        scratch_shapes=[
            vmem((ROWS, 1536), BF16),
            vmem((ROWS, LAT + ROPE), BF16),
            vmem((2, LAT + ROPE, KEYS), BF16),
            vmem((COLS, 1536), BF16),
            vmem((HEADS, 8, 128), BF16),
            vmem((HEADS, 8, 128), BF16),
            vmem((2, WIDTH, HALF * 128), BF16),
            vmem((128, 1536), BF16),
            vmem((128, COLS), BF16),
            vmem((8, 8, 16), BF16),
            vmem((128, 128), BF16),
            vmem((8, 8, 16), BF16),
            vmem((128, 128), BF16),
            vmem((HEADS, 16, 128), BF16),
            vmem((HEADS, 16, 128), BF16),
            vmem((16, 16, 128), BF16),
            vmem((CTX, 16, 128), BF16),
            vmem((ROWS, 128), BF16),
            vmem((4, ROWS, 128), BF16),
            vmem((ROWS, 128), BF16),
            vmem((16, 128), BF16),
            vmem((CHIPS, ROWS, 128), BF16),
            vmem((HALF, 16, 128), BF16),
            vmem((16, 4 * REQ, 128), BF16),
            vmem((CHIPS, 4 * REQ, 128), BF16),
            vmem((HALF, 2, 128), F32),
            vmem((CHIPS, 2, 128), F32),
            vmem((128, 128), F32),
            vmem((16, 16, 128), BF16),
            vmem((2, GROUPS, 4, 128), F32),
            vmem((2 * GROUPS, 4, 128), F32),
            pltpu.SemaphoreType.REGULAR,
            pltpu.SemaphoreType.DMA((13,)),
            pltpu.SemaphoreType.DMA((12,)),
            pltpu.SemaphoreType.DMA((20,)),
        ],
        compiler_params=pltpu.CompilerParams(
            collective_id=0, has_side_effects=True, vmem_limit_bytes=60 * 2**20
        ),
        name="latent_attention",
    )(*operands, request_adapter, group_first_request, group_request_count)


def solution(mesh):
    placed = (
        P(),
        P(),
        P("ctx", None),
        P(None, ("head", "ctx")),
        P("head", None, "ctx"),
        P("head", "ctx", None),
        P("head", "ctx"),
        P(),
        P(None, None, ("head", "ctx")),
        P(None, "ctx", None),
        P(None, None, "head"),
        P(None, "ctx", None),
        P(None, None, "head"),
        P(),
        P(),
        P(),
    )
    return jax.shard_map(
        body, mesh=mesh, in_specs=placed, out_specs=P("head", None, "ctx"), check_vma=False
    )
```

```python
import functools
import math

import jax
import jax.numpy as jnp
from jax import lax
from jax.experimental import pallas as pl
from jax.experimental.pallas import tpu as pltpu
from jax.sharding import PartitionSpec as P

MESH = pl.DeviceIdType.MESH
F32 = jnp.float32
BF16 = jnp.bfloat16

CTX = 64
CHIPS = CTX // 2
GROUPS = 8
HEADS = 16
HALF = HEADS // 2
ROWS = 32
REQ = 16
NOPE = 128
ROPE = 64
LAT = 512
COLS = 48
KEYS = 512
WIDTH = 112
PAIRS = 4
SCALE = 1.0 / math.sqrt(NOPE + ROPE)


def mm(a, b):
    return lax.dot_general(a, b, (((1,), (0,)), ((), ())), preferred_element_type=F32)


def mm_t(a, b):
    return lax.dot_general(a, b, (((1,), (1,)), ((), ())), preferred_element_type=F32)


def far_first(i, size):
    return size // 2 + ((i + 1) >> 1) * (1 - 2 * (i & 1))


def kernel(
    x_hbm,
    fresh_hbm,
    cache_hbm,
    wq_hbm,
    kup_hbm,
    vup_hbm,
    wo_hbm,
    aqd_hbm,
    aqu_hbm,
    akd_hbm,
    aku_hbm,
    avd_hbm,
    avu_hbm,
    adapter_s,
    first_s,
    count_s,
    out_ref,
    x_v,
    fresh_v,
    cache_v,
    wq_v,
    kup_v,
    vup_v,
    wo_v,
    aqd_v,
    aqu_v,
    akd_v,
    aku_v,
    avd_v,
    avu_v,
    kmsg,
    vmsg,
    kw,
    vw,
    col_s,
    qcol,
    lq_s,
    pe_s,
    lat,
    pos,
    acc_s,
    acc_r,
    ml_s,
    ml_r,
    turned,
    att,
    part,
    part_r,
    ready,
    load_sem,
    send_sem,
    recv_sem,
):
    me = lax.axis_index("ctx")
    group = lax.axis_index("head")
    chip = me >> 1
    core = me & 1
    x_at = me >> 4
    z_at = chip & 7
    place = me & 15
    head_made = me >> 2
    piece = me & 3
    head_up = 4 * (place & 3) + (place >> 2)
    up_core = head_up >> 3
    head_own = (chip ^ 4) >> 1
    block_own = (chip & 15) ^ 4
    step_own = chip & 1
    owner = core == chip >> 4

    def chip_at(i):
        dz = far_first(i >> 2, 8)
        dx = far_first(i & 3, 4)
        return (((x_at + dx) & 3) << 3) | ((z_at + dz) & 7)

    def group_of(z_there, pair):
        step = (pair - (z_there >> 1)) & 3
        nearer = 3 - 2 * (z_there & 1)
        beside = jnp.where(step == nearer, 1, 2)
        return jnp.where(step == 0, 0, jnp.where(step == 2, 3, beside))

    barrier = pltpu.get_barrier_semaphore()

    def greet(ctx, y):
        pl.semaphore_signal(barrier, inc=1, device_id=(ctx, y), device_id_type=MESH)

    def greet_plane(i, carry):
        z = (z_at + far_first(i, 8)) & 7
        greet(16 * x_at + 2 * z + core, group)
        greet(16 * x_at + 2 * z + 1 - core, group)
        return carry

    lax.fori_loop(0, 7, greet_plane, 0)
    line = [16 * ((x_at + d) & 3) + place for d in (2, 1, 3)]
    for ctx in line:
        greet(ctx, group)

    @pl.when(head_up >> 2 != x_at)
    def _():
        for n in range(4):
            greet(4 * head_up + n, group)

    def greet_group(i, carry):
        y = (group + far_first(i, GROUPS)) & (GROUPS - 1)
        greet(me, y)
        greet(me ^ 1, y)
        return carry

    lax.fori_loop(0, GROUPS - 1, greet_group, 0)
    greet(me ^ 1, group)

    up_col = pl.multiple_of(head_up * NOPE, NOPE)
    own_col = pl.multiple_of(head_own * NOPE, NOPE)
    half_col = pl.multiple_of(core * (HALF * NOPE), HALF * NOPE)
    other_col = pl.multiple_of((1 - core) * (HALF * NOPE), HALF * NOPE)
    pending = {}
    for n, (name, src, dst) in enumerate(
        (
            ("x", x_hbm, x_v),
            ("aqd", aqd_hbm, aqd_v),
            ("wq", wq_hbm, wq_v),
            ("aqu", aqu_hbm, aqu_v),
            ("kup", kup_hbm, kup_v),
            ("akd", akd_hbm, akd_v),
            ("vup", vup_hbm, vup_v),
            ("avd", avd_hbm, avd_v),
            ("aku", aku_hbm.at[:, pl.ds(up_col, NOPE)], aku_v),
            ("cache", cache_hbm, cache_v.at[0]),
            ("fresh", fresh_hbm, fresh_v),
            ("avu", avu_hbm.at[:, pl.ds(own_col, NOPE)], avu_v),
            ("wo", wo_hbm.at[:, pl.ds(half_col, HALF * NOPE)], wo_v.at[0]),
        )
    ):
        load = pltpu.make_async_copy(src, dst, load_sem.at[n])
        load.start()
        pending[name] = load.wait

    def wait(*names):
        for name in names:
            pending.pop(name)()

    def finish():
        wait(*list(pending))

    def send(src, dst, n, ctx, y, out=None):
        return pltpu.make_async_remote_copy(
            src_ref=src,
            dst_ref=dst,
            send_sem=send_sem.at[n if out is None else out],
            recv_sem=recv_sem.at[n],
            device_id=(ctx, y),
            device_id_type=MESH,
        )

    def send_or_keep(src, dst, n, ctx, y=None, out=None):
        y = group if y is None else y
        here = jnp.logical_and(ctx == me, y == group)

        @pl.when(here)
        def _():
            pltpu.make_async_copy(src, dst, recv_sem.at[n]).start()

        @pl.when(jnp.logical_not(here))
        def _():
            send(src, dst, n, ctx, y, out).start()

    def arrives(name, ref, n, when=None):
        wait_all = pltpu.make_async_copy(ref, ref, recv_sem.at[n]).wait
        pending[name] = wait_all if when is None else lambda: pl.when(when)(wait_all)

    def leaves(name, ref, n, kept=None, fewer=None):
        wait_all = pltpu.make_async_copy(ref, ref, send_sem.at[n]).wait

        def either():
            pl.when(kept)(pltpu.make_async_copy(fewer, fewer, send_sem.at[n]).wait)
            pl.when(jnp.logical_not(kept))(wait_all)

        pending[name] = wait_all if kept is None else either

    lane_adapter = lax.broadcasted_iota(jnp.int32, (REQ, 128), 1) // 16
    request = lax.broadcasted_iota(jnp.int32, (REQ, 128), 0)
    adapter = jnp.zeros((REQ, 128), jnp.int32)
    first = jnp.zeros((REQ, 128), jnp.int32)
    count = jnp.zeros((REQ, 128), jnp.int32)
    for r in range(REQ):
        adapter = jnp.where(request == r, adapter_s[r], adapter)
    for a in range(8):
        first = jnp.where(lane_adapter == a, first_s[a], first)
        count = jnp.where(lane_adapter == a, count_s[a], count)
    owns = adapter == lane_adapter
    within = request - first
    live = jnp.logical_and(owns, jnp.logical_and(within >= 0, within < count))
    own_mask = jnp.where(owns, 1.0, 0.0).astype(F32)
    live_mask = jnp.where(live, 1.0, 0.0).astype(F32)
    live_mask = jnp.concatenate([live_mask, live_mask], axis=0)

    wait("x", "aqd")
    x = x_v[...]
    low = (mm_t(x, aqd_v[...]) * live_mask).astype(BF16)
    wait("wq", "aqu")
    cols = (mm_t(x, wq_v[...]) + mm(low, aqu_v[...])).astype(BF16)
    col_s[...] = jnp.concatenate(
        [cols.astype(F32), jnp.zeros((ROWS, 128 - COLS), F32)], axis=1
    ).astype(BF16)

    wait("kup", "akd")
    table = jnp.concatenate([akd_v[a].astype(F32) for a in range(8)], axis=1)
    for h in range(HEADS):
        kmsg[h] = jnp.concatenate([kup_v[h].astype(F32), table], axis=0).astype(BF16)

    pl.semaphore_wait(barrier, 15 + 3 + 3 + 2 * (GROUPS - 1))
    for ctx in line:
        pl.semaphore_signal(ready, inc=1, device_id=(ctx, group), device_id_type=MESH)
    pending["ready"] = lambda: pl.semaphore_wait(ready, 3)

    def send_keys(i, carry):
        z = (z_at + far_first(i, 8)) & 7
        for c in range(2):
            to = 2 * z + c
            src = kmsg.at[4 * (to & 3) + (to >> 2)]
            send(src, kw.at[place], 0, 16 * x_at + to, group).start()
        return carry

    lax.fori_loop(0, 7, send_keys, 0)
    to = place ^ 1
    src = kmsg.at[4 * (to & 3) + (to >> 2)]
    send(src, kw.at[place], 0, me ^ 1, group).start()
    pltpu.make_async_copy(kmsg.at[head_up], kw.at[place], recv_sem.at[0]).start()
    arrives("kw", kw, 0)
    leaves("kw out", kw.at[pl.ds(0, 15)], 0)

    to = ((head_made & 3) << 2) | (head_made >> 2)
    for i in range(4):
        send_or_keep(
            col_s, qcol.at[piece], 2, 16 * ((x_at + (2, 1, 3, 0)[i]) & 3) + to
        )
    arrives("qcol", qcol, 2)
    leaves("qcol out", qcol, 2, piece == x_at, qcol.at[pl.ds(0, 3)])

    wait("qcol")
    q0 = qcol[0].astype(F32)
    q1 = qcol[1].astype(F32)
    q2 = qcol[2].astype(F32)
    q3 = qcol[3].astype(F32)
    nope = jnp.concatenate([q0[:, :48], q1[:, :48], q2[:, :32]], axis=1).astype(BF16)
    pe = jnp.concatenate([q2[:, 32:48], q3[:, :48]], axis=1)
    pe_s[...] = jnp.concatenate([pe[:16], pe[16:]], axis=1).astype(BF16)

    wait("ready")

    def send_pe(i, carry):
        z = (z_at + far_first(i, 8)) & 7
        n = 12 + 2 * group_of(z, z_at >> 1)
        send_or_keep(
            pe_s, pos.at[head_up & 7], n, 16 * x_at + 2 * z + up_core, out=4
        )
        return carry

    lax.fori_loop(0, 8, send_pe, 0)
    for n in range(PAIRS):
        arrives("pos %d" % n, pos.at[pl.ds(0, HALF // PAIRS)], 12 + 2 * n)
    leaves("pos out", pos, 4, core == up_core, pos.at[pl.ds(0, 7)])

    wait("aku")
    low_key = (mm_t(nope, aku_v[...]) * live_mask).astype(BF16)
    wait("kw")
    kwf = kw[...].astype(F32)
    key_up = kwf[:, :8].reshape(128, 128).astype(BF16)
    key_down = kwf[:, 8:].reshape(128, 128).astype(BF16)
    lq_s[...] = (mm_t(nope, key_up) + mm_t(low_key, key_down)).astype(BF16)

    slot = (head_up & 7) * 4 + x_at

    def send_lat(i, carry):
        there = chip_at(i)
        n = 11 + 2 * group_of(there & 7, z_at >> 1)
        send(lq_s, lat.at[slot], n, 2 * there + up_core, group, out=5).start()
        return carry

    def send_lat_far(i, carry):
        z = (z_at + far_first(i, 8)) & 7
        to = 16 * x_at + 2 * z + up_core
        send(lq_s, lat.at[slot], 19, to, group, out=5).start()
        return carry

    lax.fori_loop(0, 3, send_lat_far, 0)
    lax.fori_loop(12, CHIPS - 1, send_lat, 0)
    send_or_keep(lq_s, lat.at[slot], 11, 2 * chip + up_core, out=5)
    leaves("lat out", lat.at[pl.ds(0, 23)], 5, core == up_core, lat.at[pl.ds(0, 22)])
    for n in range(2):
        arrives("lat %d" % n, lat.at[pl.ds(0, 8)], 11 + 2 * n)
    arrives("lat 3", lat.at[pl.ds(0, 6)], 17)
    facing = (z_at & 1) == core
    six = lat.at[pl.ds(0, 6)]
    eight = lat.at[pl.ds(0, 8)]

    def wait_beside():
        pl.when(facing)(pltpu.make_async_copy(eight, eight, recv_sem.at[15]).wait)
        pl.when(jnp.logical_not(facing))(
            pltpu.make_async_copy(six, six, recv_sem.at[15]).wait
        )

    pending["lat 2"] = wait_beside

    share = send(cache_hbm, cache_v.at[1], 1, me ^ 1, group)
    share.start()
    pending["share"] = share.wait_recv
    pending["share out"] = share.wait_send

    wait("vup", "avd")
    table = jnp.concatenate([avd_v[a].astype(F32) for a in range(8)], axis=1)
    for h in range(HEADS):
        vmsg[h] = jnp.concatenate([vup_v[h].astype(F32), table], axis=0).astype(BF16)

    def send_values(i, carry):
        there = chip_at(i)
        send(
            vmsg.at[(there ^ 4) >> 1], vw.at[me], 3, 2 * there + (there >> 4), group
        ).start()
        return carry

    lax.fori_loop(0, CHIPS - 1, send_values, 0)
    send_or_keep(vmsg.at[head_own], vw.at[me], 3, 2 * chip + (chip >> 4))
    arrives("vw", vw, 3, owner)
    leaves(
        "vw out", vw.at[pl.ds(0, CHIPS)], 3, owner, vw.at[pl.ds(0, CHIPS - 1)]
    )

    def pass_on(*steps):
        came = lat.at[pl.ds(0, 2 * len(steps))]
        pltpu.make_async_copy(came, came, recv_sem.at[19]).wait()
        for step in steps:
            z = (z_at + step) & 7
            for c in range(2):
                made = 4 * ((2 * z + c) & 3) + (z >> 1)
                row = (made & 7) * 4 + x_at
                n = 11 + 2 * group_of(z_at, z >> 1)
                for dx in (2, 1, 3):
                    to = 16 * ((x_at + dx) & 3) + 2 * z_at + core
                    send(lat.at[row], lat.at[row], n, to, group, out=11).start()

    pl.when(facing)(lambda: pass_on(4))
    pl.when(jnp.logical_not(facing))(lambda: pass_on(3, 5))
    leaves("passed out", lat.at[pl.ds(0, 12)], 11, facing, lat.at[pl.ds(0, 6)])

    next_pair = 2 * (z_at & 1) - 1
    pairs = [((z_at >> 1) + d) & 3 for d in (0, next_pair, -next_pair, 2)]

    def owner_of(block):
        return 2 * (16 * core + (block ^ 4)) + core

    for n_pair in range(PAIRS):
        heads = [pairs[n_pair], pairs[n_pair] + 4]
        wait("pos %d" % n_pair, "lat %d" % n_pair)
        q_lat = jnp.concatenate(
            [
                jnp.concatenate([lat[4 * h + j] for j in range(4)], axis=1)
                for h in heads
            ],
            axis=0,
        )
        q_pe = []
        for h in heads:
            both = pos[h].astype(F32)
            q_pe += [both[:, :ROPE], both[:, ROPE:]]
        q_pe = jnp.concatenate(q_pe, axis=0).astype(BF16)
        if n_pair == 0:
            wait("cache", "share")
        scores = [
            (mm(q_lat, cache_v[n, :LAT]) + mm(q_pe, cache_v[n, LAT:])) * SCALE
            for n in range(2)
        ]
        top = jnp.maximum(
            jnp.max(scores[0], axis=1, keepdims=True),
            jnp.max(scores[1], axis=1, keepdims=True),
        )
        weights = [jnp.exp(s - top) for s in scores]
        total = jnp.sum(weights[0], axis=1, keepdims=True) + jnp.sum(
            weights[1], axis=1, keepdims=True
        )
        lane = lax.broadcasted_iota(jnp.int32, (2 * ROWS, 128), 1)
        stats = jnp.where(lane == 0, top, jnp.where(lane == 1, total, 0.0))
        stats = jnp.concatenate([stats, stats], axis=0).T[:2]
        for n, h in enumerate(heads):
            ml_s[h] = stats if n == 0 else pltpu.roll(stats, 128 - 32 * n, 1)

        for h in heads:
            for step in range(2):
                send_or_keep(ml_s.at[h], ml_r.at[chip], 6, owner_of(2 * h + step))

        summed = sum(mm_t(weights[n].astype(BF16), cache_v[n, :LAT]) for n in range(2))
        for n, h in enumerate(heads):
            for step in range(2):
                rows = summed[32 * n + 16 * step : 32 * n + 16 * step + 16]
                for j in range(4):
                    acc_s[2 * h + step, 16 * j : 16 * j + 16] = rows[
                        :, 128 * j : 128 * j + 128
                    ].astype(BF16)

        for h in heads:
            for step in range(2):
                block = 2 * h + step
                send_or_keep(acc_s.at[block], acc_r.at[chip], 7, owner_of(block))

    arrives("ml", ml_r, 6, owner)
    leaves("ml out", ml_r.at[pl.ds(0, 16)], 6, owner, ml_r.at[pl.ds(0, 15)])
    arrives("acc", acc_r, 7, owner)
    leaves("acc out", acc_r.at[pl.ds(0, 16)], 7, owner, acc_r.at[pl.ds(0, 15)])

    share = send(
        wo_hbm.at[:, pl.ds(other_col, HALF * NOPE)], wo_v.at[1], 10, me ^ 1, group
    )
    share.start()
    pending["wo share"] = share.wait_recv
    pending["wo share out"] = share.wait_send

    wait("fresh", "avu")
    for name in ("vw", "ml", "acc"):
        pending.pop(name)

    def arrived(ref, n):
        pltpu.make_async_copy(ref, ref, recv_sem.at[n]).wait()

    @pl.when(owner)
    def _():
        fresh = fresh_v[...]
        own = head_own & 7
        own_rows = pl.ds(pl.multiple_of(REQ * step_own, REQ), REQ)
        own_lat = jnp.concatenate([lat[4 * own + j, own_rows] for j in range(4)], axis=1)
        both = pos[own].astype(F32)
        own_pe = jnp.where(step_own == 0, both[:, :ROPE], both[:, ROPE:]).astype(BF16)
        own_scores = (
            mm_t(own_lat, fresh[:, :LAT]) + mm_t(own_pe, fresh[:, LAT:])
        ) * SCALE
        row = lax.broadcasted_iota(jnp.int32, (REQ, ROWS), 0)
        key = lax.broadcasted_iota(jnp.int32, (REQ, ROWS), 1)
        seen = jnp.logical_and(row == key % REQ, key // REQ <= step_own)
        own_scores = jnp.where(seen, own_scores, -jnp.inf)
        own_top = jnp.max(own_scores, axis=1, keepdims=True)
        own_weights = jnp.exp(own_scores - own_top)
        own_total = jnp.sum(own_weights, axis=1, keepdims=True)
        own_sum = mm(own_weights.astype(BF16), fresh[:, :LAT])

        arrived(vw, 3)
        vwf = vw[...].astype(F32)
        value_up = vwf[:, :8].reshape(LAT, 128).astype(BF16)
        value_down = vwf[:, 8:].reshape(LAT, 128).astype(BF16)

        arrived(ml_r, 6)
        ml = ml_r[...]
        turned[...] = jnp.concatenate(
            [ml[:, 0], ml[:, 1], jnp.zeros((64, 128), F32)], axis=0
        ).T
        stats = turned[pl.ds(pl.multiple_of(REQ * step_own, REQ), REQ), :]
        tops = stats[:, :CHIPS]
        totals = stats[:, CHIPS : 2 * CHIPS]
        joined = jnp.maximum(jnp.max(tops, axis=1, keepdims=True), own_top)
        factors = jnp.exp(tops - joined)
        own_factor = jnp.exp(own_top - joined)
        row_total = (
            jnp.sum(factors * totals, axis=1, keepdims=True) + own_factor * own_total
        )
        latent = own_sum * own_factor
        latent = [latent[:, 128 * j : 128 * j + 128] for j in range(4)]
        arrived(acc_r, 7)
        for n in range(CHIPS):
            factor = factors[:, n : n + 1]
            for j in range(4):
                got = acc_r[n, REQ * j : REQ * j + REQ].astype(F32)
                latent[j] = latent[j] + factor * got
        latent = jnp.concatenate(latent, axis=1) / row_total

        high = latent.astype(BF16)
        rest = latent - high.astype(F32)
        middle = rest.astype(BF16)
        low = (rest - middle.astype(F32)).astype(BF16)
        parts = jnp.concatenate([high, middle, low], axis=0)
        value = mm(parts, value_up)
        low_value = mm(parts, value_down)
        value = value[:16] + value[16:32] + value[32:48]
        low_value = low_value[:16] + low_value[16:32] + low_value[32:48]
        low_value = (low_value * own_mask).astype(BF16)
        att[block_own] = (value + mm(low_value, avu_v[...])).astype(BF16)


    @pl.when(owner)
    def _():
        def send_att(i, carry):
            send(
                att.at[block_own], att.at[block_own], 8, 2 * chip_at(i) + core, group
            ).start()
            return carry

        lax.fori_loop(0, CHIPS - 1, send_att, 0)

    wait("wo", "wo share")
    all_here = pltpu.make_async_copy(att, att, recv_sem.at[8]).wait
    but_own = att.at[pl.ds(0, 15)]
    pl.when(owner)(pltpu.make_async_copy(but_own, but_own, recv_sem.at[8]).wait)
    pl.when(jnp.logical_not(owner))(all_here)
    many = vw.at[pl.ds(0, CHIPS - 1)]
    all_sent = pltpu.make_async_copy(many, many, send_sem.at[8]).wait
    pending["att out"] = lambda: pl.when(owner)(all_sent)
    rows = jnp.concatenate(
        [
            jnp.concatenate([att[2 * h], att[2 * h + 1]], axis=0)
            for h in range(HALF)
        ],
        axis=1,
    )
    for n in range(2):
        mixed = mm_t(rows, wo_v[n])
        mixed = jnp.concatenate([mixed, jnp.zeros((ROWS, 128 - WIDTH), F32)], axis=1)
        for y in range(GROUPS):
            part[n, y] = jnp.concatenate(
                [mixed[2 * y : 2 * y + 2], mixed[REQ + 2 * y : REQ + 2 * y + 2]], axis=0
            )

    def send_part(i, carry):
        y = (group + far_first(i, GROUPS)) & (GROUPS - 1)
        for n in range(2):
            send(part.at[n, y], part_r.at[2 * group + core], 9, me ^ n, y).start()
        return carry

    lax.fori_loop(0, GROUPS - 1, send_part, 0)
    send(part.at[1, group], part_r.at[2 * group + core], 9, me ^ 1, group).start()
    pltpu.make_async_copy(
        part.at[0, group], part_r.at[2 * group + core], recv_sem.at[9]
    ).start()
    finish()
    arrives("part", part_r, 9)
    leaves("part out", part_r.at[pl.ds(0, 2 * GROUPS - 1)], 9)
    wait("part")
    done = part_r[0]
    for n in range(1, 2 * GROUPS):
        done = done + part_r[n]
    done = done[:, :WIDTH].astype(BF16)
    for step in range(2):
        for r in range(2):
            out_ref[r, step : step + 1, :] = done[2 * step + r : 2 * step + r + 1]

    finish()


def body(
    normed_query_latent,
    fresh_token_latent,
    prefix_latent_cache,
    query_up_weight,
    key_up_weight,
    value_up_weight,
    output_weight,
    adapter_query_down,
    adapter_query_up,
    adapter_key_down,
    adapter_key_up,
    adapter_value_down,
    adapter_value_up,
    request_adapter,
    group_first_request,
    group_request_count,
):
    operands = (
        normed_query_latent.reshape(ROWS, -1),
        fresh_token_latent.reshape(ROWS, -1),
        prefix_latent_cache.T,
        query_up_weight.T,
        jnp.transpose(key_up_weight, (0, 2, 1)),
        value_up_weight,
        output_weight.T,
        jnp.transpose(adapter_query_down, (0, 2, 1)).reshape(128, -1),
        adapter_query_up.reshape(128, COLS),
        adapter_key_down,
        adapter_key_up.reshape(128, -1),
        adapter_value_down,
        adapter_value_up.reshape(128, -1),
    )
    vmem = pltpu.VMEM
    return pl.pallas_call(
        kernel,
        out_shape=jax.ShapeDtypeStruct((2, 2, WIDTH), BF16),
        in_specs=[pl.BlockSpec(memory_space=pl.ANY)] * 13
        + [pl.BlockSpec(memory_space=pltpu.SMEM)] * 3,
        out_specs=pl.BlockSpec(memory_space=pltpu.VMEM),
        scratch_shapes=[
            vmem((ROWS, 1536), BF16),
            vmem((ROWS, LAT + ROPE), BF16),
            vmem((2, LAT + ROPE, KEYS), BF16),
            vmem((COLS, 1536), BF16),
            vmem((HEADS, 8, 128), BF16),
            vmem((HEADS, 8, 128), BF16),
            vmem((2, WIDTH, HALF * 128), BF16),
            vmem((128, 1536), BF16),
            vmem((128, COLS), BF16),
            vmem((8, 8, 16), BF16),
            vmem((128, 128), BF16),
            vmem((8, 8, 16), BF16),
            vmem((128, 128), BF16),
            vmem((HEADS, 16, 128), BF16),
            vmem((HEADS, 16, 128), BF16),
            vmem((16, 16, 128), BF16),
            vmem((CTX, 16, 128), BF16),
            vmem((ROWS, 128), BF16),
            vmem((4, ROWS, 128), BF16),
            vmem((ROWS, 128), BF16),
            vmem((16, 128), BF16),
            vmem((CHIPS, ROWS, 128), BF16),
            vmem((HALF, 16, 128), BF16),
            vmem((16, 4 * REQ, 128), BF16),
            vmem((CHIPS, 4 * REQ, 128), BF16),
            vmem((HALF, 2, 128), F32),
            vmem((CHIPS, 2, 128), F32),
            vmem((128, 128), F32),
            vmem((16, 16, 128), BF16),
            vmem((2, GROUPS, 4, 128), F32),
            vmem((2 * GROUPS, 4, 128), F32),
            pltpu.SemaphoreType.REGULAR,
            pltpu.SemaphoreType.DMA((13,)),
            pltpu.SemaphoreType.DMA((12,)),
            pltpu.SemaphoreType.DMA((20,)),
        ],
        compiler_params=pltpu.CompilerParams(
            collective_id=0, has_side_effects=True, vmem_limit_bytes=60 * 2**20
        ),
        name="latent_attention",
    )(*operands, request_adapter, group_first_request, group_request_count)


def solution(mesh):
    placed = (
        P(),
        P(),
        P("ctx", None),
        P(None, ("head", "ctx")),
        P("head", None, "ctx"),
        P("head", "ctx", None),
        P("head", "ctx"),
        P(),
        P(None, None, ("head", "ctx")),
        P(None, "ctx", None),
        P(None, None, "head"),
        P(None, "ctx", None),
        P(None, None, "head"),
        P(),
        P(),
        P(),
    )
    return jax.shard_map(
        body, mesh=mesh, in_specs=placed, out_specs=P("head", None, "ctx"), check_vma=False
    )
```
